256 devices in a mesh: dp: 16 (over y, x_hi, core), seq: 16 (over x_lo, z).
Axes of the slice: x: 4 (x_hi: 2, x_lo: 2; x = x_hi * 2 + x_lo), y: 4, z: 8, core: 2. Of those that a mesh axis runs over, the one named last changes fastest.
Arguments:
- proj_inputs: bfloat16 [16, 2048, 2560], P('dp', 'seq'), may hold values from -6 to 6
- queries: bfloat16 [16, 2048, 4096], P('dp', 'seq'), may hold values from -140 to 140
- key_state_rows: bfloat16 [16, 2048, 512], P('dp', 'seq'), may hold values from -5 to 5
- value_state_rows: bfloat16 [16, 2048, 512], P('dp', 'seq'), may hold values from -6 to 6
- d_out: bfloat16 [16, 2048, 4096], P('dp', 'seq'), may hold values from -6 to 6
- w_tiles: bfloat16 [320, 128, 128], P('seq', 'dp'), may hold values from -0.15625 to 0.15625
- tile_rows: int32 [32, 10], replicated, may hold values from 0 to 19, as said below
- loss_scale: int32 [1], replicated, may hold values from 64 to 256
Outputs:
- d_x: bfloat16 [16, 2048, 2560], P('dp', 'seq')
- d_k: bfloat16 [16, 2048, 512], P('dp', 'seq')
- d_v: bfloat16 [16, 2048, 512], P('dp', 'seq')
- d_w: float32 [320, 128, 128], P('seq', 'dp')
The draws below stay inside these ranges and needn't reach their ends.
Inputs may be any that keep to these rules, and one draw needn't show every extreme that they name: `tile_rows`: each row lists 10 distinct row tiles out of 20, in increasing order.
All inputs are finite; a program needn't handle non-finite values.
Results may differ from the reference program's by a relative error of at most 0.035.
Values may be sent and summed in bfloat16 or wider, within the bound.
A program may use at most 128 MiB of HBM per device.

```python
import jax
import jax.numpy as jnp
from jax import lax

D = 2560
QUERY_HEADS = 32
KEY_VALUE_HEADS = 4
HEAD_WIDTH = 128
TILE = 128
KEEP = 10
RTILES = 20
NCB = 32
NTILES = 320
SEQUENCE_LENGTH = 2048
BATCH_SEQUENCES = 16


def shared_keys(key):
    base_offset = jnp.clip(jax.random.normal(key, (BATCH_SEQUENCES, SEQUENCE_LENGTH, KEY_VALUE_HEADS * HEAD_WIDTH), jnp.float32), -5.0, 5.0)
    return base_offset


def draw_key_state_rows(key, part):
    base_offset = shared_keys(key)
    return base_offset.astype(jnp.bfloat16)


def draw_queries(key, part):
    key = jax.random.fold_in(key, 7)
    own = jnp.clip(jax.random.normal(key, (BATCH_SEQUENCES, SEQUENCE_LENGTH, QUERY_HEADS * HEAD_WIDTH), jnp.float32), -5.0, 5.0)
    return own.astype(jnp.bfloat16)


def draw_tile_rows(key, part):
    key = jax.random.fold_in(key, 11)
    block_keys = jax.random.split(key, NCB)
    orders = jax.vmap(lambda one_key: jax.random.permutation(one_key, RTILES))(block_keys)
    return jnp.sort(orders[:, :KEEP], axis=1).astype(jnp.int32)


def block_levels(rng, dims, cuts, smallest, largest):
    level, own = 1.0, jax.random.fold_in(rng, 6)
    for axis_at, blocks in cuts:
        heights = jnp.exp(jax.random.uniform(jax.random.fold_in(own, axis_at), (blocks,), jnp.float32, smallest / len(cuts), largest / len(cuts)))
        level = level * jnp.repeat(heights, dims[axis_at] // blocks).reshape([-1 if axis == axis_at else 1 for axis in range(len(dims))])
    return level


def normal_values(own_key, extent, deviation, most, cuts=(), kind=jnp.bfloat16):
    array = deviation * jax.random.normal(own_key, extent, jnp.float32)
    if cuts:
        array = array * block_levels(own_key, extent, cuts, -0.22, 0.18)
    return jnp.clip(array, -most, most).astype(kind)


def setup_inputs(seed: int = 0) -> dict:
    keys = jax.random.split(jax.random.key(seed), 9)
    return {
        "proj_inputs": normal_values(keys[0], (BATCH_SEQUENCES, SEQUENCE_LENGTH, D), 1.0, 6.0, ((0, 16), (1, 16))),
        "queries": draw_queries(jax.random.fold_in(keys[8], 71), 0),
        "key_state_rows": draw_key_state_rows(jax.random.fold_in(keys[8], 71), 0),
        "value_state_rows": normal_values(keys[3], (BATCH_SEQUENCES, SEQUENCE_LENGTH, KEY_VALUE_HEADS * HEAD_WIDTH), 1.0, 6.0, ((0, 16), (1, 16))),
        "d_out": normal_values(keys[4], (BATCH_SEQUENCES, SEQUENCE_LENGTH, QUERY_HEADS * HEAD_WIDTH), 1.0, 6.0, ((0, 16), (1, 16))),
        "w_tiles": normal_values(keys[5], (NTILES, TILE, TILE), (D // 2) ** -0.5, 0.15625, ((0, 16), (1, 16))),
        "tile_rows": draw_tile_rows(jax.random.fold_in(keys[8], 71), 0),
        "loss_scale": jax.random.randint(keys[7], (1,), 64, 257).astype(jnp.int32),
    }


def tile_picker(tile_rows):
    return (tile_rows[:, :, None] == jnp.arange(RTILES, dtype=jnp.int32)[None, None, :]).astype(jnp.float32)


def dense_weight(w_tiles, tile_rows):
    tiles = w_tiles.reshape(NCB, KEEP, TILE, TILE).astype(jnp.float32)
    dense = jnp.einsum('ckr,ckij->ricj', tile_picker(tile_rows), tiles, precision=lax.Precision.HIGHEST)
    return dense.reshape(D, NCB * TILE).astype(jnp.bfloat16)


def head_group(inputs):
    q_group, k_head, v_head, grad_group = inputs
    softmax_scale = HEAD_WIDTH ** -0.5
    q_float = q_group.astype(jnp.float32)
    k_float = k_head.astype(jnp.float32)
    v_float = v_head.astype(jnp.float32)
    grad_float = grad_group.astype(jnp.float32)
    scores = jnp.einsum('qnd,kd->nqk', q_float, k_float) * softmax_scale
    positions = jnp.arange(SEQUENCE_LENGTH, dtype=jnp.int32)
    causal = positions[None, :] <= positions[:, None]
    scores = jnp.where(causal[None], scores, -1e30)
    row_top = jnp.max(scores, axis=-1, keepdims=True)
    expo = jnp.exp(scores - row_top)
    probs = expo / jnp.sum(expo, axis=-1, keepdims=True)
    probs_low = lax.optimization_barrier(probs.astype(jnp.bfloat16)).astype(jnp.float32)
    dprobs = jnp.einsum('qnd,kd->nqk', grad_float, v_float)
    row_delta = jnp.sum(probs_low * dprobs, axis=-1, keepdims=True)
    dscores = lax.optimization_barrier((probs * (dprobs - row_delta)).astype(jnp.bfloat16)).astype(jnp.float32)
    dq_group = (jnp.einsum('nqk,kd->qnd', dscores, k_float) * softmax_scale).astype(jnp.bfloat16)
    dk_head = jnp.einsum('nqk,qnd->kd', dscores, q_float) * softmax_scale
    dv_head = jnp.einsum('nqk,qnd->kd', probs_low, grad_float)
    return dq_group, dk_head, dv_head


def sequence_grads(inputs):
    query_sequence, key_sequence, value_sequence, output_grad_sequence = inputs
    query_group = QUERY_HEADS // KEY_VALUE_HEADS
    query_head_rows = query_sequence.reshape(SEQUENCE_LENGTH, KEY_VALUE_HEADS, query_group, HEAD_WIDTH).transpose(1, 0, 2, 3)
    output_grad_heads = output_grad_sequence.reshape(SEQUENCE_LENGTH, KEY_VALUE_HEADS, query_group, HEAD_WIDTH).transpose(1, 0, 2, 3)
    key_head_rows = key_sequence.reshape(SEQUENCE_LENGTH, KEY_VALUE_HEADS, HEAD_WIDTH).transpose(1, 0, 2)
    value_head_rows = value_sequence.reshape(SEQUENCE_LENGTH, KEY_VALUE_HEADS, HEAD_WIDTH).transpose(1, 0, 2)
    dq_heads, key_grad_heads, value_grad_heads = lax.map(head_group, (query_head_rows, key_head_rows, value_head_rows, output_grad_heads))
    dq_seq = dq_heads.transpose(1, 0, 2, 3).reshape(SEQUENCE_LENGTH, QUERY_HEADS * HEAD_WIDTH)
    key_grad_sequence = key_grad_heads.transpose(1, 0, 2).reshape(SEQUENCE_LENGTH, KEY_VALUE_HEADS * HEAD_WIDTH).astype(jnp.bfloat16)
    value_grad_sequence = value_grad_heads.transpose(1, 0, 2).reshape(SEQUENCE_LENGTH, KEY_VALUE_HEADS * HEAD_WIDTH).astype(jnp.bfloat16)
    return dq_seq, key_grad_sequence, value_grad_sequence


def reference(proj_inputs, queries, key_state_rows, value_state_rows, d_out, w_tiles, tile_rows, loss_scale):
    dq_all, d_k, d_v = lax.map(sequence_grads, (queries, key_state_rows, value_state_rows, d_out))
    w_dense = dense_weight(w_tiles, tile_rows)
    flat_dq = dq_all.reshape(BATCH_SEQUENCES * SEQUENCE_LENGTH, QUERY_HEADS * HEAD_WIDTH)
    d_x = jnp.dot(flat_dq, w_dense.T, preferred_element_type=jnp.float32).astype(jnp.bfloat16)
    d_x = d_x.reshape(BATCH_SEQUENCES, SEQUENCE_LENGTH, D)
    full_grad = jnp.dot(proj_inputs.reshape(BATCH_SEQUENCES * SEQUENCE_LENGTH, D).T, flat_dq, preferred_element_type=jnp.float32)
    picked = jnp.einsum('ckr,ricj->ckij', tile_picker(tile_rows), full_grad.reshape(RTILES, TILE, NCB, TILE), precision=lax.Precision.HIGHEST)
    d_w = picked.reshape(NTILES, TILE, TILE) / loss_scale[0].astype(jnp.float32)
    return d_x, d_k, d_v, d_w
```

```python
import functools

import jax
import jax.numpy as jnp
from jax import lax
from jax.experimental import pallas as pl
from jax.experimental.pallas import tpu as pltpu
from jax.sharding import PartitionSpec as P

D = 2560
W = 128
KEEP = 10
RTILES = 20
ZN = 8
HALF = 2048
HP = 4
R = HP * W
CK = 256
SCALE = W**-0.5
EXP_SCALE = SCALE * 1.4426950408889634
MESH = pl.DeviceIdType.MESH
F32 = jnp.float32
BF16 = jnp.bfloat16


def dot_t(a, b):
    return lax.dot_general(a, b, (((1,), (1,)), ((), ())), preferred_element_type=F32)


def dot(a, b):
    return lax.dot_general(a, b, (((1,), (0,)), ((), ())), preferred_element_type=F32)


def fold(x, op):
    return op(x.reshape(x.shape[0] // 8, 8, x.shape[1]), axis=0)


def attend(g, blk, head, z, qbuf, dobuf, kbuf, vbuf, kt, acc, e_scr, dp_scr, q_s, do_s, dq_t, dq_ref):
    for i in range(HP):
        cols = pl.ds(pl.multiple_of((head + i) * W, W), W)
        q_s[i * W : (i + 1) * W, :] = qbuf[blk, :, cols]
        do_s[i * W : (i + 1) * W, :] = dobuf[blk, :, cols]
    t = blk * ZN + z
    full = t // 2

    def chunk(ref, c):
        return ref[g, c // 4, pl.ds((c % 4) * 2, 2)].reshape(CK, W)

    def rows(c):
        return pl.ds(pl.multiple_of(c * CK, CK), CK)

    def scores(c, top):
        s = dot_t(chunk(kbuf, c), q_s[...])
        e_scr[rows(c), :] = s
        return jnp.maximum(top, fold(s, jnp.max))

    top = lax.fori_loop(0, full, scores, jnp.full((8, R), -1e30, F32))
    s = dot_t(chunk(kbuf, full), q_s[...])
    key = full * CK + lax.broadcasted_iota(jnp.int32, (CK, R), 0)
    pos = t * W + lax.broadcasted_iota(jnp.int32, (CK, R), 1) % W
    s = jnp.where(key <= pos, s, -1e30)
    e_scr[rows(full), :] = s
    top = jnp.max(jnp.maximum(top, fold(s, jnp.max)), axis=0, keepdims=True)

    def exps(c, carry):
        total, weighted = carry
        e = jnp.exp2((e_scr[rows(c), :] - top) * EXP_SCALE)
        dp = dot_t(chunk(vbuf, c), do_s[...])
        e_scr[rows(c), :] = e
        dp_scr[rows(c), :] = dp
        return total + fold(e, jnp.sum), weighted + fold(e * dp, jnp.sum)

    zero = jnp.zeros((8, R), F32)
    total, weighted = lax.fori_loop(0, full + 1, exps, (zero, zero))
    inv = 1.0 / jnp.sum(total, axis=0, keepdims=True)
    delta = jnp.sum(weighted, axis=0, keepdims=True) * inv
    dq_t[...] = jnp.zeros_like(dq_t)

    def grads(c, carry):
        p = e_scr[rows(c), :] * inv
        ds = (p * (dp_scr[rows(c), :] - delta)).astype(BF16)
        acc[0, g, rows(c), :] += dot(ds, q_s[...])
        acc[1, g, rows(c), :] += dot(p.astype(BF16), do_s[...])
        dq_t[...] += dot(kt[g, :, pl.ds(pl.multiple_of(c * CK, CK), CK)], ds)
        return carry

    lax.fori_loop(0, full + 1, grads, 0)
    for i in range(HP):
        cols = pl.ds(pl.multiple_of((head + i) * W, W), W)
        dq_ref[blk, :, cols] = (dq_t[:, i * W : (i + 1) * W] * SCALE).T.astype(BF16)


def attention_kernel(
    q_ref, do_ref, k_ref, v_ref, dq_ref, dk_ref, dv_ref,
    qbuf, dobuf, kbuf, vbuf, kt, acc, e_scr, dp_scr, q_s, do_s, dq_t,
    out_r, in_r, out_l, in_l, swap_out, swap_in,
    own_sem, kv_send, kv_recv, q_send, q_recv, ring_send, ring_recv,
    rs_send, rs_recv, swap_send, swap_recv,
):
    s = lax.axis_index("seq")
    h, z = s // ZN, s % ZN
    partner = (1 - h) * ZN + z
    right = h * ZN + (z + 1) % ZN
    left = h * ZN + (z + ZN - 1) % ZN
    barrier = pltpu.get_barrier_semaphore()
    for d in (partner, right, left):
        pl.semaphore_signal(barrier, inc=1, device_id={"seq": d}, device_id_type=MESH)
    pl.semaphore_wait(barrier, 3)

    def remote(src, dst, ssem, rsem, d):
        return pltpu.make_async_remote_copy(src, dst, ssem, rsem, device_id={"seq": d}, device_id_type=MESH)

    def cols(start, size):
        return pl.ds(pl.multiple_of(start, W), size)

    swaps, own = [], []
    for kv, (src, buf) in enumerate(((k_ref, kbuf), (v_ref, vbuf))):
        for g in range(2):
            swaps.append(
                remote(src.at[:, cols(((1 - h) * 2 + g) * W, W)], buf.at[g, h, z],
                       kv_send.at[kv, g], kv_recv.at[kv, g], partner))
            own.append(pltpu.make_async_copy(
                src.at[:, cols((h * 2 + g) * W, W)], buf.at[g, h, z], own_sem.at[kv, g]))
    for c in swaps:
        c.start()
    for c in own:
        c.start()
    q_copies, q_own = [], []
    for g in range(2):
        for i, (src, buf) in enumerate(((q_ref, qbuf), (do_ref, dobuf))):
            part = pl.ds(g * 1024, 1024)
            q_copies.append(remote(src.at[:, cols((1 - h) * HALF + g * 1024, 1024)], buf.at[h, :, part],
                                   q_send.at[g, i], q_recv.at[g, i], partner))
            q_own.append(pltpu.make_async_copy(
                src.at[:, cols(h * HALF + g * 1024, 1024)], buf.at[h, :, part], own_sem.at[2 + g, i]))
    for c in q_copies:
        c.start()
    for c in q_own:
        c.start()
    acc[...] = jnp.zeros_like(acc)

    def ring(kv, way, step):
        buf = (kbuf, vbuf)[kv]
        if way == 0:
            at, to = (z + ZN - step) % ZN, right
        else:
            at, to = (z + step) % ZN, left
        return remote(buf.at[:, :, at], buf.at[:, :, at], ring_send.at[kv, way, step], ring_recv.at[kv, way, step], to)

    hops = ((4, 3), (3, 4))
    for c in own:
        c.wait()
    for kv in range(2):
        for g in range(2):
            swaps[kv * 2 + g].wait_recv()
        for way in range(2):
            ring(kv, way, 0).start()
    for step in range(4):
        for kv in range(2):
            for way in range(2):
                if step < hops[kv][way]:
                    ring(kv, way, step).wait_recv()
                    if step + 1 < hops[kv][way]:
                        ring(kv, way, step + 1).start()

    def turn(b, carry):
        kt[b // 16, :, cols((b % 16) * W, W)] = kbuf[b // 16, (b % 16) // ZN, b % ZN].T
        return carry

    lax.fori_loop(0, 32, turn, 0)
    for c in q_own:
        c.wait()

    def package(g, d):
        return [[acc[kv, g, pl.ds(pl.multiple_of((hl * ZN + d) * W, W), W), :] * (SCALE if kv == 0 else 1.0)
                 for hl in range(2)] for kv in range(2)]

    def rs(g, way, step):
        src, dst, to = ((out_r, in_r, right), (out_l, in_l, left))[way]
        return remote(src.at[g, step], dst.at[g, step], rs_send.at[g, way, step], rs_recv.at[g, way, step], to)

    def rs_step(g, step):
        for way, n in ((0, 4), (1, 3)):
            if step >= n:
                continue
            src, dst = ((out_r, in_r), (out_l, in_l))[way]
            d = (z + 4 - step) % ZN if way == 0 else (z + ZN - 3 + step) % ZN
            part = package(g, d)
            if step > 0:
                rs(g, way, step - 1).wait_recv()
            for kv in range(2):
                for hl in range(2):
                    v = part[kv][hl]
                    if step > 0:
                        v = v + dst[g, step - 1, kv, hl].astype(F32)
                    src[g, step, kv, hl] = v.astype(BF16)
            rs(g, way, step).start()

    def pair(g):
        return remote(swap_out.at[g], swap_in.at[g], swap_send.at[g], swap_recv.at[g], partner)

    def rs_end(g):
        part = package(g, z)
        rs(g, 0, 3).wait_recv()
        rs(g, 1, 2).wait_recv()
        for kv, out in enumerate((dk_ref, dv_ref)):
            both = [part[kv][hl] + in_r[g, 3, kv, hl].astype(F32) + in_l[g, 2, kv, hl].astype(F32) for hl in range(2)]
            mine = jnp.where(h == 0, both[0], both[1])
            other = jnp.where(h == 0, both[1], both[0])
            out[:, cols((h * 2 + g) * W, W)] = mine.astype(BF16)
            swap_out[g, kv] = other.astype(BF16)
        pair(g).start()

    def rs_out(g):
        pair(g).wait_recv()
        for kv, out in enumerate((dk_ref, dv_ref)):
            out[:, cols(((1 - h) * 2 + g) * W, W)] = swap_in[g, kv]

    per_g = 16 // HP

    def work(it, carry):
        g = it // per_g
        rest = it % per_g
        second = rest // (per_g // 2)
        blk = jnp.where(second == 0, h, 1 - h)
        head = g * 8 + (rest % (per_g // 2)) * HP
        for gg in range(2):

            @pl.when(it == gg * per_g + per_g // 2)
            def _():
                for i in range(2):
                    q_copies[gg * 2 + i].wait_recv()

        for step in range(4):

            @pl.when(it == per_g + step)
            def _():
                rs_step(0, step)

        attend(g, blk, head, z, qbuf, dobuf, kbuf, vbuf, kt, acc, e_scr, dp_scr, q_s, do_s, dq_t, dq_ref)
        return carry

    lax.fori_loop(0, 2 * per_g, work, 0)
    rs_step(1, 0)
    rs_end(0)
    for step in range(1, 4):
        rs_step(1, step)
    rs_out(0)
    rs_end(1)
    rs_out(1)
    for c in swaps + q_copies:
        c.wait_send()
    for kv in range(2):
        for way in range(2):
            for step in range(hops[kv][way]):
                ring(kv, way, step).wait_send()
    for g in range(2):
        for way, n in ((0, 4), (1, 3)):
            for step in range(n):
                rs(g, way, step).wait_send()
        pair(g).wait_send()


def attention(q, do, k, v):
    any_spec = pl.BlockSpec(memory_space=pl.ANY)
    vmem = pl.BlockSpec(memory_space=pltpu.VMEM)
    dma = pltpu.SemaphoreType.DMA
    return pl.pallas_call(
        attention_kernel,
        out_shape=(
            jax.ShapeDtypeStruct((2, W, HALF), BF16),
            jax.ShapeDtypeStruct((W, 512), BF16),
            jax.ShapeDtypeStruct((W, 512), BF16),
        ),
        in_specs=[any_spec] * 4,
        out_specs=(vmem, vmem, vmem),
        scratch_shapes=[
            pltpu.VMEM((2, W, HALF), BF16),
            pltpu.VMEM((2, W, HALF), BF16),
            pltpu.VMEM((2, 2, ZN, W, W), BF16),
            pltpu.VMEM((2, 2, ZN, W, W), BF16),
            pltpu.VMEM((2, W, 2048), BF16),
            pltpu.VMEM((2, 2, 2048, W), F32),
            pltpu.VMEM((2048, R), F32),
            pltpu.VMEM((2048, R), F32),
            pltpu.VMEM((R, W), BF16),
            pltpu.VMEM((R, W), BF16),
            pltpu.VMEM((W, R), F32),
            pltpu.VMEM((2, 4, 2, 2, W, W), BF16),
            pltpu.VMEM((2, 4, 2, 2, W, W), BF16),
            pltpu.VMEM((2, 3, 2, 2, W, W), BF16),
            pltpu.VMEM((2, 3, 2, 2, W, W), BF16),
            pltpu.VMEM((2, 2, W, W), BF16),
            pltpu.VMEM((2, 2, W, W), BF16),
            dma((4, 2)),
            dma((2, 2)),
            dma((2, 2)),
            dma((2, 2)),
            dma((2, 2)),
            dma((2, 2, 4)),
            dma((2, 2, 4)),
            dma((2, 2, 4)),
            dma((2, 2, 4)),
            dma((2,)),
            dma((2,)),
        ],
        compiler_params=pltpu.CompilerParams(
            collective_id=0, has_side_effects=True, vmem_limit_bytes=48 * 2**20
        ),
        cost_estimate=pl.CostEstimate(flops=10 * 10**9, bytes_accessed=8 * 10**6, transcendentals=10**7),
    )(q, do, k, v)


def project_kernel(inv_ref, rows_ref, dq_ref, x_ref, w_ref, dx_ref, dw_ref, xt, wcat):
    for r in range(RTILES):
        xt[r] = x_ref[:, :, r * W : (r + 1) * W].reshape(2 * W, W).T

    def weights(c, carry):
        dq_c = dq_ref[:, :, pl.ds(pl.multiple_of(c * W, W), W)].reshape(2 * W, W)
        xs = jnp.concatenate([xt[rows_ref[c * KEEP + k]] for k in range(KEEP)], axis=0)
        out = dot(xs, dq_c).astype(BF16)
        dw_ref[pl.ds(c * KEEP, KEEP)] = out.reshape(KEEP, W, W)
        return carry

    lax.fori_loop(0, 16, weights, 0)

    def inputs(r2, carry):
        for i in range(2):
            for c in range(16):
                k = inv_ref[(r2 * 2 + i) * 16 + c]
                tile = w_ref[c * KEEP + jnp.minimum(k, KEEP - 1)]
                wcat[i * W : (i + 1) * W, c * W : (c + 1) * W] = jnp.where(k < KEEP, tile, jnp.zeros_like(tile))
        out = dot_t(dq_ref[...].reshape(2 * W, HALF), wcat[...]).astype(BF16)
        dx_ref[:, :, pl.ds(pl.multiple_of(r2 * 2 * W, 2 * W), 2 * W)] = out.reshape(2, W, 2 * W)
        return carry

    lax.fori_loop(0, RTILES // 2, inputs, 0)


def project(inv, rows, dq, x, w):
    vmem = pl.BlockSpec(memory_space=pltpu.VMEM)
    smem = pl.BlockSpec(memory_space=pltpu.SMEM)
    return pl.pallas_call(
        project_kernel,
        out_shape=(
            jax.ShapeDtypeStruct((2, W, D), BF16),
            jax.ShapeDtypeStruct((16 * KEEP, W, W), BF16),
        ),
        in_specs=[smem, smem, vmem, vmem, vmem],
        out_specs=(vmem, vmem),
        scratch_shapes=[
            pltpu.VMEM((RTILES, W, 2 * W), BF16),
            pltpu.VMEM((2 * W, HALF), BF16),
        ],
        compiler_params=pltpu.CompilerParams(vmem_limit_bytes=48 * 2**20),
        cost_estimate=pl.CostEstimate(flops=4 * 10**9, bytes_accessed=15 * 10**6, transcendentals=0),
    )(inv, rows, dq, x, w)


def body(x, q, k, v, do, w, tile_rows, loss_scale):
    s = lax.axis_index("seq")
    h = s // ZN
    halves = [list(range(ZN)), list(range(ZN, 2 * ZN))]
    cross = [(i, (i + ZN) % (2 * ZN)) for i in range(2 * ZN)]
    w_all = lax.all_gather(w, "dp", axis=1, tiled=True)
    w_half = lax.all_gather(w_all, "seq", axis=0, tiled=True, axis_index_groups=halves)
    x_other = lax.ppermute(x[0], "seq", cross)
    x_pair = jnp.where(h == 0, jnp.stack([x[0], x_other]), jnp.stack([x_other, x[0]]))
    my_rows = lax.dynamic_slice_in_dim(tile_rows, h * 16, 16, 0)
    hit = my_rows[:, :, None] == jnp.arange(RTILES, dtype=jnp.int32)
    inv = jnp.min(jnp.where(hit, jnp.arange(KEEP, dtype=jnp.int32)[None, :, None], KEEP), axis=1).T.reshape(-1)

    dq, dk, dv = attention(q[0], do[0], k[0], v[0])
    dx_pair, dw_part = project(inv, my_rows.reshape(-1), dq, x_pair, w_half)
    dx_mine = lax.dynamic_index_in_dim(dx_pair, h, 0, keepdims=False)
    dx_theirs = lax.dynamic_index_in_dim(dx_pair, 1 - h, 0, keepdims=False)
    dx_got = lax.ppermute(dx_theirs, "seq", cross)
    dx = (dx_mine.astype(F32) + dx_got.astype(F32)).astype(BF16)
    dw = lax.psum_scatter(dw_part, "dp", scatter_dimension=1, tiled=True)
    dw = lax.psum_scatter(dw, "seq", scatter_dimension=0, tiled=True, axis_index_groups=halves)
    dw = dw.astype(F32) / loss_scale[0].astype(F32)
    return dx[None], dk[None], dv[None], dw


def solution(mesh):
    tokens = P("dp", "seq", None)
    tiles = P("seq", "dp", None)
    return jax.shard_map(
        body,
        mesh=mesh,
        in_specs=(tokens,) * 5 + (tiles, P(), P()),
        out_specs=(tokens, tokens, tokens, tiles),
        check_vma=False,
    )
```

```python
import functools

import jax
import jax.numpy as jnp
from jax import lax
from jax.experimental import pallas as pl
from jax.experimental.pallas import tpu as pltpu
from jax.sharding import PartitionSpec as P

D = 2560
W = 128
KEEP = 10
RTILES = 20
ZN = 8
HALF = 2048
HP = 4
R = HP * W
CK = 512
KB = CK // W
YN = 4
TZ = 20
SCALE = W**-0.5
VMEM_LIMIT = 60 * 2**20
EXP_SCALE = SCALE * 1.4426950408889634
MESH = pl.DeviceIdType.MESH
F32 = jnp.float32
BF16 = jnp.bfloat16


def dot_t(a, b):
    return lax.dot_general(a, b, (((1,), (1,)), ((), ())), preferred_element_type=F32)


def dot(a, b):
    return lax.dot_general(a, b, (((1,), (0,)), ((), ())), preferred_element_type=F32)


def fold(x, op):
    return op(x.reshape(x.shape[0] // 8, 8, x.shape[1]), axis=0)


def attend(g, blk, head, z, qbuf, dobuf, kv, kt, acc, e_scr, dp_scr, q_s, do_s, dq_t, dq_ref):
    for i in range(HP):
        cols = pl.ds(pl.multiple_of((head + i) * W, W), W)
        q_s[i * W : (i + 1) * W, :] = qbuf[blk, :, cols]
        do_s[i * W : (i + 1) * W, :] = dobuf[blk, :, cols]
    t = blk * ZN + z
    full = t // KB

    def chunk(ref, c):
        return kv[ref, g, c // (ZN // KB), pl.ds((c % (ZN // KB)) * KB, KB)].reshape(CK, W)

    def rows(c):
        return pl.ds(pl.multiple_of(c * CK, CK), CK)

    def scores(c, top):
        s = dot_t(chunk(0, c), q_s[...])
        e_scr[rows(c), :] = s
        return jnp.maximum(top, fold(s, jnp.max))

    top = lax.fori_loop(0, full, scores, jnp.full((8, R), -1e30, F32))
    s = dot_t(chunk(0, full), q_s[...])
    key = full * CK + lax.broadcasted_iota(jnp.int32, (CK, R), 0)
    pos = t * W + lax.broadcasted_iota(jnp.int32, (CK, R), 1) % W
    s = jnp.where(key <= pos, s, -1e30)
    e_scr[rows(full), :] = s
    top = jnp.max(jnp.maximum(top, fold(s, jnp.max)), axis=0, keepdims=True)

    def exps(c, carry):
        total, weighted = carry
        e = jnp.exp2((e_scr[rows(c), :] - top) * EXP_SCALE)
        dp = dot_t(chunk(1, c), do_s[...])
        e_scr[rows(c), :] = e
        dp_scr[rows(c), :] = dp
        return total + fold(e, jnp.sum), weighted + fold(e * dp, jnp.sum)

    zero = jnp.zeros((8, R), F32)
    total, weighted = lax.fori_loop(0, full + 1, exps, (zero, zero))
    inv = 1.0 / jnp.sum(total, axis=0, keepdims=True)
    delta = jnp.sum(weighted, axis=0, keepdims=True) * inv
    dq_t[...] = jnp.zeros_like(dq_t)

    def grads(c, carry):
        p = e_scr[rows(c), :] * inv
        ds = (p * (dp_scr[rows(c), :] - delta)).astype(BF16)
        acc[0, g, rows(c), :] += dot(ds, q_s[...])
        acc[1, g, rows(c), :] += dot(p.astype(BF16), do_s[...])
        dq_t[...] += dot(kt[g, :, pl.ds(pl.multiple_of(c * CK, CK), CK)], ds)
        return carry

    lax.fori_loop(0, full + 1, grads, 0)
    for i in range(HP):
        cols = pl.ds(pl.multiple_of((head + i) * W, W), W)
        dq_ref[blk, :, cols] = (dq_t[:, i * W : (i + 1) * W] * SCALE).T.astype(BF16)


def fused_kernel(
    inv_ref, rows_ref, x_ref, q_ref, k_ref, v_ref, do_ref, w_ref,
    dx_ref, dk_ref, dv_ref, dw_ref,
    qbuf, dobuf, kv, kt, acc, e_scr, dp_scr, q_s, do_s, dq_t, dq,
    xbuf, xt, wg, wt, wcat, dws, core_in, y_in, s2, z_in, xh_out, xh_in,
    dx_own, dx_out, dx_in, out_r, in_r, out_l, in_l, swap_out, swap_in,
    own_sem, kv_send, kv_recv, q_send, q_recv, x_send, x_recv,
    ring_send, ring_recv, wx_send, wx_recv, wz_send, wz_recv, wy_send, wy_recv, wc_send, wc_recv,
    rs_send, rs_recv, swap_send, swap_recv, c_send, c_recv, y_send, y_recv, z_send, z_recv,
    xh_send, xh_recv, dx_send, dx_recv,
):
    s = lax.axis_index("seq")
    dp = lax.axis_index("dp")
    h, z = s // ZN, s % ZN
    y, xh, core = dp // 4, (dp // 2) % 2, dp % 2
    partner = {"seq": (1 - h) * ZN + z}
    right = {"seq": h * ZN + (z + 1) % ZN}
    left = {"seq": h * ZN + (z + ZN - 1) % ZN}
    y_peer = [{"dp": (y + j) % YN * 4 + xh * 2 + core} for j in range(1, YN)]
    xh_peer = {"dp": y * 4 + (1 - xh) * 2 + core}
    core_peer = {"dp": y * 4 + xh * 2 + 1 - core}
    z_peer = [{"seq": h * ZN + (z + j) % ZN} for j in range(1, ZN)]
    barrier = pltpu.get_barrier_semaphore()
    peers = [partner, xh_peer, core_peer] + y_peer + z_peer
    for d in peers:
        pl.semaphore_signal(barrier, inc=1, device_id=d, device_id_type=MESH)

    def remote(src, dst, ssem, rsem, d):
        return pltpu.make_async_remote_copy(src, dst, ssem, rsem, device_id=d, device_id_type=MESH)

    def cols(start, size):
        return pl.ds(pl.multiple_of(start, W), size)

    own = []

    def local(src, dst):
        c = pltpu.make_async_copy(src, dst, own_sem.at[len(own)])
        c.start()
        own.append(c)

    for g in range(2):
        for i, src in enumerate((k_ref, v_ref)):
            local(src.at[:, cols((h * 2 + g) * W, W)], kv.at[i, g, h, z])
    local(w_ref, wg.at[core, y, z, xh])
    local(x_ref, xbuf.at[h])
    for g in range(2):
        for src, buf in ((q_ref, qbuf), (do_ref, dobuf)):
            local(src.at[:, cols(h * HALF + g * 1024, 1024)], buf.at[h, :, pl.ds(g * 1024, 1024)])
    pl.semaphore_wait(barrier, len(peers))

    swaps = []
    for g in range(2):
        swaps.append([remote(src.at[:, cols(((1 - h) * 2 + g) * W, W)], kv.at[i, g, h, z],
                             kv_send.at[g, i], kv_recv.at[g, i], partner) for i, src in enumerate((k_ref, v_ref))])
    q_copies = []
    for g in range(2):
        q_copies.append([remote(src.at[:, cols((1 - h) * HALF + g * 1024, 1024)], buf.at[h, :, pl.ds(g * 1024, 1024)],
                                q_send.at[g, i], q_recv.at[g, i], partner)
                         for i, (src, buf) in enumerate(((q_ref, qbuf), (do_ref, dobuf)))])
    x_copy = remote(x_ref, xbuf.at[h], x_send, x_recv, partner)
    wx = remote(w_ref, wg.at[core, y, z, xh], wx_send, wx_recv, xh_peer)
    for c in swaps[0] + [wx] + swaps[1] + q_copies[0] + [x_copy] + q_copies[1]:
        c.start()

    def ring_at(way, step):
        return ((z + ZN - step) % ZN, right) if way == 0 else ((z + step) % ZN, left)

    def ring(g, way, step):
        at, to = ring_at(way, step)
        ref = kv.at[way, g, :, at] if step == 3 else kv.at[:, g, :, at]
        return remote(ref, ref, ring_send.at[g, way, step], ring_recv.at[g, way, step], to)

    def wring(way, step):
        at, to = ring_at(way, step)
        ref = wg.at[core, y, at, way] if step == 3 else wg.at[core, y, at]
        return remote(ref, ref, wz_send.at[way, step], wz_recv.at[way, step], to)

    def to_y(at, j):
        ref = wg.at[core, y, at]
        return remote(ref, ref, wy_send.at[at, j], wy_recv.at[at, j], y_peer[j])

    def ring_start(g):
        for i in range(2):
            swaps[g][i].wait_recv()
        for way in range(2):
            ring(g, way, 0).start()

    def ring_step(g, step):
        for way in range(2):
            ring(g, way, step).wait_recv()
            if step < 3:
                ring(g, way, step + 1).start()

    def w_start():
        wx.wait_recv()
        for way in range(2):
            wring(way, 0).start()
        for j in range(3):
            to_y(z, j).start()

    def w_step(step):
        for way in range(2):
            wring(way, step).wait_recv()
            if step < 3:
                wring(way, step + 1).start()
                for j in range(3):
                    to_y((z + ZN - 1 - step) % ZN if way == 0 else (z + 1 + step) % ZN, j).start()
        if step == 3:
            for j in range(3):
                to_y((z + 4) % ZN, j).start()

    w_core = remote(wg.at[core], wg.at[core], wc_send, wc_recv, core_peer)

    def w_swap():
        def one(i, carry):
            for j in range(3):
                to_y(i, j).wait_recv()
            return carry

        lax.fori_loop(0, ZN, one, 0)
        w_core.start()

    def turn_keys(g):
        def one(b, carry):
            kt[g, :, cols(b * W, W)] = kv[0, g, b // ZN, b % ZN].T
            return carry

        lax.fori_loop(0, 2 * ZN, one, 0)

    def turn_x(blk):
        def one(r, carry):
            xt[r, blk] = xbuf[blk, :, cols(r * W, W)].T
            return carry

        lax.fori_loop(0, RTILES, one, 0)

    acc[...] = jnp.zeros_like(acc)
    for c in own[:4]:
        c.wait()
    ring_start(0)
    own[4].wait()
    own[5].wait()
    turn_x(h)
    for step in range(4):
        ring_step(0, step)
    ring_start(1)
    turn_keys(0)
    for c in own[6:]:
        c.wait()

    def package(g, d):
        return [[acc[i, g, cols((hl * ZN + d) * W, W), :] * (SCALE if i == 0 else 1.0)
                 for hl in range(2)] for i in range(2)]

    def rs(g, way, step):
        src, dst, to = ((out_r, in_r, right), (out_l, in_l, left))[way]
        return remote(src.at[g, step], dst.at[g, step], rs_send.at[g, way, step], rs_recv.at[g, way, step], to)

    def rs_step(g, step):
        for way, n in ((0, 4), (1, 3)):
            if step >= n:
                continue
            src, dst = ((out_r, in_r), (out_l, in_l))[way]
            d = (z + 4 - step) % ZN if way == 0 else (z + ZN - 3 + step) % ZN
            part = package(g, d)
            if step > 0:
                rs(g, way, step - 1).wait_recv()
            for i in range(2):
                for hl in range(2):
                    v = part[i][hl]
                    if step > 0:
                        v = v + dst[g, step - 1, i, hl].astype(F32)
                    src[g, step, i, hl] = v.astype(BF16)
            rs(g, way, step).start()

    def pair(g):
        return remote(swap_out.at[g], swap_in.at[g], swap_send.at[g], swap_recv.at[g], partner)

    def rs_end(g):
        part = package(g, z)
        rs(g, 0, 3).wait_recv()
        rs(g, 1, 2).wait_recv()
        for i, out in enumerate((dk_ref, dv_ref)):
            both = [part[i][hl] + in_r[g, 3, i, hl].astype(F32) + in_l[g, 2, i, hl].astype(F32) for hl in range(2)]
            mine = jnp.where(h == 0, both[0], both[1])
            other = jnp.where(h == 0, both[1], both[0])
            out[:, cols((h * 2 + g) * W, W)] = mine.astype(BF16)
            swap_out[g, i] = other.astype(BF16)
        pair(g).start()

    def rs_out(g):
        pair(g).wait_recv()
        for i, out in enumerate((dk_ref, dv_ref)):
            out[:, cols(((1 - h) * 2 + g) * W, W)] = swap_in[g, i]

    def dw_tiles(p):
        for c4 in range(4):
            c = p * 4 + c4
            xs = jnp.concatenate(
                [jnp.concatenate([xt[rows_ref[c * KEEP + k], b] for b in range(2)], axis=1) for k in range(KEEP)], axis=0)
            out = dot(xs, dq[:, :, cols(c * W, W)].reshape(2 * W, W))
            out = out.reshape(KEEP, YN, 2, 2, 8, W)
            for cc in range(2):
                for yy in range(YN):
                    dws[p, cc, yy, c4 // 2, pl.ds((c4 % 2) * KEEP, KEEP)] = (
                        out[:, yy, :, cc].reshape(KEEP, 16, W).astype(BF16))
        to_core(p).start()

    def to_core(p):
        return remote(dws.at[p, 1 - core], core_in.at[p], c_send.at[p], c_recv.at[p], core_peer)

    def dw_y(p, j):
        return remote(dws.at[p, core, (y + j + 1) % YN], y_in.at[p, j], y_send.at[p, j], y_recv.at[p, j], y_peer[j])

    def dw_to_y(p):
        to_core(p).wait_recv()
        for j in (1, 0, 2):
            yy = (y + j + 1) % YN
            dws[p, core, yy] = (dws[p, core, yy].astype(F32) + core_in[p, yy].astype(F32)).astype(BF16)
            dw_y(p, j).start()
        dws[p, core, y] = (dws[p, core, y].astype(F32) + core_in[p, y].astype(F32)).astype(BF16)

    def dw_z(p, i):
        return remote(s2.at[p, i], z_in.at[z], z_send.at[p, i], z_recv.at[z], {"seq": h * ZN + p * 2 + i})

    def dw_to_z(p):
        for j in range(3):
            dw_y(p, j).wait_recv()
        for i in range(2):
            v = dws[p, core, y, i].astype(F32)
            for j in range(3):
                v = v + y_in[p, j, i].astype(F32)
            s2[p, i] = v.astype(BF16)

            @pl.when(p * 2 + i != z)
            def _():
                dw_z(p, i).start()

    xh_copy = remote(xh_out, xh_in, xh_send, xh_recv, xh_peer)

    def dw_to_x():
        z_in[z] = s2[z // 2, z % 2]
        for i in range(ZN):

            @pl.when(i != z)
            def _():
                remote(z_in.at[i], z_in.at[i], z_send.at[0, 0], z_recv.at[i], partner).wait_recv()

        total = z_in[0].astype(F32)
        for i in range(1, ZN):
            total = total + z_in[i].astype(F32)
        low, high = total[:, :8], total[:, 8:]
        dw_ref[...] = jnp.where(xh == 0, low, high)
        xh_out[...] = jnp.where(xh == 0, high, low)
        xh_copy.start()

    def dw_end():
        xh_copy.wait_recv()
        dw_ref[...] += xh_in[...]

    def when(cond, f):
        pl.when(cond)(f)

    def work(it, carry):
        g = it // 4
        blk = jnp.where(it % 2 == 0, h, 1 - h)
        head = it // 2 * HP
        for i in range(4):
            when(it == i, functools.partial(ring_step, 1, i))
            when(it == 4 + i, functools.partial(rs_step, 0, i))
            when(it == 1 + i, functools.partial(w_step, i))
        when(it == 0, w_start)
        when(it == 7, w_swap)
        for gg in range(2):

            @pl.when(it == gg * 4 + 1)
            def _():
                for c in q_copies[gg]:
                    c.wait_recv()

        @pl.when(it == 2)
        def _():
            x_copy.wait_recv()
            turn_x(1 - h)

        when(it == 4, functools.partial(turn_keys, 1))

        @pl.when((it % 2 == 0) & (it > 1))
        def _():
            dw_tiles(it // 2 - 1)

        @pl.when((it % 2 == 1) & (it > 2))
        def _():
            dw_to_y(it // 2 - 1)

        @pl.when((it % 2 == 1) & (it > 4))
        def _():
            dw_to_z(it // 2 - 2)

        attend(g, blk, head, z, qbuf, dobuf, kv, kt, acc, e_scr, dp_scr, q_s, do_s, dq_t, dq)
        return carry

    lax.fori_loop(0, 8, work, 0)

    def assemble(i, carry):
        zz, m = i // (TZ // 2), i % (TZ // 2)
        v = wg[:, :, zz, :, pl.ds(pl.multiple_of(m * 16, 16), 16), :].astype(F32).reshape(2, YN, 2, 2, 8, W)
        v = v.transpose(3, 1, 2, 0, 4, 5).reshape(2, W, W)
        wt[pl.ds(zz * TZ + m * 2, 2)] = v.astype(BF16)
        return carry

    def dx_part(r2):
        part = cols(r2 * 2 * W, 2 * W)
        return remote(dx_out.at[:, part], dx_in.at[:, part], dx_send.at[r2], dx_recv.at[r2], partner)

    def dx_step(r2, carry):
        for i in range(2):
            for c in range(16):
                k = inv_ref[(r2 * 2 + i) * 16 + c]
                tile = wt[c * KEEP + jnp.minimum(k, KEEP - 1)]
                wcat[i * W : (i + 1) * W, c * W : (c + 1) * W] = jnp.where(k < KEEP, tile, jnp.zeros_like(tile))
        part = cols(r2 * 2 * W, 2 * W)
        out = dot_t(dq[...].reshape(2 * W, HALF), wcat[...])
        first, second = out[:W], out[W:]
        dx_out[:, part] = jnp.where(h == 0, second, first).astype(BF16)
        dx_part(r2).start()
        dx_own[:, part] = jnp.where(h == 0, first, second)
        return carry

    def dx_end(r2, carry):
        dx_part(r2).wait_recv()
        part = cols(r2 * 2 * W, 2 * W)
        dx_ref[:, part] = (dx_own[:, part] + dx_in[:, part].astype(F32)).astype(BF16)
        return carry

    dw_tiles(3)
    rs_step(1, 0)
    rs_end(0)
    dw_to_z(2)
    dw_to_y(3)
    rs_step(1, 1)
    w_core.wait_recv()
    lax.fori_loop(0, ZN * TZ // 2, assemble, 0)
    rs_step(1, 2)
    lax.fori_loop(0, 4, dx_step, 0)
    rs_step(1, 3)
    dw_to_z(3)
    lax.fori_loop(4, 10, dx_step, 0)
    rs_end(1)
    dw_to_x()
    rs_out(0)
    rs_out(1)
    lax.fori_loop(0, 10, dx_end, 0)
    dw_end()

    for c in swaps[0] + swaps[1] + q_copies[0] + q_copies[1] + [x_copy, wx, w_core, xh_copy]:
        c.wait_send()
    for way in range(2):
        for step in range(4):
            ring(0, way, step).wait_send()
            ring(1, way, step).wait_send()
            wring(way, step).wait_send()
    for g in range(2):
        for way, n in ((0, 4), (1, 3)):
            for step in range(n):
                rs(g, way, step).wait_send()
        pair(g).wait_send()

    def sent_w(i, carry):
        for j in range(3):
            to_y(i, j).wait_send()
        return carry

    lax.fori_loop(0, ZN, sent_w, 0)

    def sent_dw(p, carry):
        to_core(p).wait_send()
        for j in range(3):
            dw_y(p, j).wait_send()
        for i in range(2):

            @pl.when(p * 2 + i != z)
            def _():
                dw_z(p, i).wait_send()

        return carry

    lax.fori_loop(0, 4, sent_dw, 0)

    def sent_dx(r2, carry):
        dx_part(r2).wait_send()
        return carry

    lax.fori_loop(0, 10, sent_dx, 0)


def fused(inv, rows, x, q, k, v, do, w):
    any_spec = pl.BlockSpec(memory_space=pl.ANY)
    vmem = pl.BlockSpec(memory_space=pltpu.VMEM)
    smem = pl.BlockSpec(memory_space=pltpu.SMEM)
    dma = pltpu.SemaphoreType.DMA

    def low(*shape):
        return pltpu.VMEM(shape, BF16)

    def full(*shape):
        return pltpu.VMEM(shape, F32)

    return pl.pallas_call(
        fused_kernel,
        out_shape=(
            jax.ShapeDtypeStruct((W, D), BF16),
            jax.ShapeDtypeStruct((W, 512), BF16),
            jax.ShapeDtypeStruct((W, 512), BF16),
            jax.ShapeDtypeStruct((TZ, 8, W), F32),
        ),
        in_specs=[smem] * 2 + [any_spec] * 6,
        out_specs=(vmem,) * 4,
        scratch_shapes=[
            low(2, W, HALF), low(2, W, HALF), low(2, 2, 2, ZN, W, W), low(2, W, 2048), full(2, 2, 2048, W),
            full(2048, R), full(2048, R), low(R, W), low(R, W), full(W, R), low(2, W, HALF),
            low(2, W, D), low(RTILES, 2, W, W), low(2, YN, ZN, 2, TZ * 8, W), low(ZN * TZ, W, W), low(2 * W, HALF),
            low(4, 2, YN, 2, TZ, 16, W), low(4, YN, 2, TZ, 16, W), low(4, 3, 2, TZ, 16, W), low(4, 2, TZ, 16, W),
            low(ZN, TZ, 16, W), full(TZ, 8, W), full(TZ, 8, W),
            full(W, D), low(W, D), low(W, D),
            low(2, 4, 2, 2, W, W), low(2, 4, 2, 2, W, W), low(2, 3, 2, 2, W, W), low(2, 3, 2, 2, W, W),
            low(2, 2, W, W), low(2, 2, W, W),
            dma((10,)), dma((2, 2)), dma((2, 2)), dma((2, 2)), dma((2, 2)), dma, dma,
            dma((2, 2, 4)), dma((2, 2, 4)), dma, dma, dma((2, 4)), dma((2, 4)), dma((ZN, 3)), dma((ZN, 3)), dma, dma,
            dma((2, 2, 4)), dma((2, 2, 4)), dma((2,)), dma((2,)), dma((4,)), dma((4,)), dma((4, 3)), dma((4, 3)),
            dma((4, 2)), dma((ZN,)), dma, dma, dma((10,)), dma((10,)),
        ],
        compiler_params=pltpu.CompilerParams(
            collective_id=0, has_side_effects=True, vmem_limit_bytes=VMEM_LIMIT
        ),
        cost_estimate=pl.CostEstimate(flops=14 * 10**9, bytes_accessed=8 * 10**6, transcendentals=10**7),
    )(inv, rows, x, q, k, v, do, w)


def body(x, q, k, v, do, w, tile_rows, loss_scale):
    h = lax.axis_index("seq") // ZN
    my_rows = lax.dynamic_slice_in_dim(tile_rows, h * 16, 16, 0)
    hit = my_rows[:, :, None] == jnp.arange(RTILES, dtype=jnp.int32)
    inv = jnp.min(jnp.where(hit, jnp.arange(KEEP, dtype=jnp.int32)[None, :, None], KEEP), axis=1).T.reshape(-1)
    dx, dk, dv, dw = fused(
        inv, my_rows.reshape(-1), x[0], q[0], k[0], v[0], do[0], w.reshape(TZ * 8, W))
    return dx[None], dk[None], dv[None], dw / loss_scale[0].astype(F32)


def solution(mesh):
    tokens = P("dp", "seq", None)
    tiles = P("seq", "dp", None)
    return jax.shard_map(
        body,
        mesh=mesh,
        in_specs=(tokens,) * 5 + (tiles, P(), P()),
        out_specs=(tokens, tokens, tokens, tiles),
        check_vma=False,
    )
```

```python
import functools

import jax
import jax.numpy as jnp
from jax import lax
from jax.experimental import pallas as pl
from jax.experimental.pallas import tpu as pltpu
from jax.sharding import PartitionSpec as P

D = 2560
W = 128
KEEP = 10
RTILES = 20
ZN = 8
HALF = 2048
HP = 4
R = HP * W
CK = 512
KB = CK // W
YN = 4
HOPS = ((4, 3), (3, 4))
TZ = 20
SCALE = W**-0.5
VMEM_LIMIT = 60 * 2**20
EXP_SCALE = SCALE * 1.4426950408889634
MESH = pl.DeviceIdType.MESH
F32 = jnp.float32
BF16 = jnp.bfloat16


def dot_t(a, b):
    return lax.dot_general(a, b, (((1,), (1,)), ((), ())), preferred_element_type=F32)


def dot(a, b):
    return lax.dot_general(a, b, (((1,), (0,)), ((), ())), preferred_element_type=F32)


def fold(x, op):
    return op(x.reshape(x.shape[0] // 8, 8, x.shape[1]), axis=0)


def attend(g, blk, head, z, qbuf, dobuf, kv, kt, acc, e_scr, dp_scr, q_s, do_s, dq_t, dq_ref, tick):
    tick(0)
    for i in range(HP):
        cols = pl.ds(pl.multiple_of((head + i) * W, W), W)
        q_s[i * W : (i + 1) * W, :] = qbuf[blk, :, cols]
        do_s[i * W : (i + 1) * W, :] = dobuf[blk, :, cols]
    t = blk * ZN + z
    full = t // KB

    def chunk(ref, c):
        return kv[ref, g, c // (ZN // KB), pl.ds((c % (ZN // KB)) * KB, KB)].reshape(CK, W)

    def rows(c):
        return pl.ds(pl.multiple_of(c * CK, CK), CK)

    def scores(c, top):
        s = dot_t(chunk(0, c), q_s[...])
        e_scr[rows(c), :] = s
        return jnp.maximum(top, fold(s, jnp.max))

    top = lax.fori_loop(0, full, scores, jnp.full((8, R), -1e30, F32))
    s = dot_t(chunk(0, full), q_s[...])
    key = full * CK + lax.broadcasted_iota(jnp.int32, (CK, R), 0)
    pos = t * W + lax.broadcasted_iota(jnp.int32, (CK, R), 1) % W
    s = jnp.where(key <= pos, s, -1e30)
    e_scr[rows(full), :] = s
    top = jnp.max(jnp.maximum(top, fold(s, jnp.max)), axis=0, keepdims=True)

    tick(1)

    def exps(c, carry):
        total, weighted = carry
        e = jnp.exp2((e_scr[rows(c), :] - top) * EXP_SCALE)
        dp = dot_t(chunk(1, c), do_s[...])
        e_scr[rows(c), :] = e
        dp_scr[rows(c), :] = dp
        return total + fold(e, jnp.sum), weighted + fold(e * dp, jnp.sum)

    zero = jnp.zeros((8, R), F32)
    total, weighted = lax.fori_loop(0, full + 1, exps, (zero, zero))
    inv = 1.0 / jnp.sum(total, axis=0, keepdims=True)
    delta = jnp.sum(weighted, axis=0, keepdims=True) * inv
    dq_t[...] = jnp.zeros_like(dq_t)
    tick(2)

    def grads(c, carry):
        p = e_scr[rows(c), :] * inv
        ds = (p * (dp_scr[rows(c), :] - delta)).astype(BF16)
        acc[0, g, rows(c), :] += dot(ds, q_s[...])
        acc[1, g, rows(c), :] += dot(p.astype(BF16), do_s[...])
        dq_t[...] += dot(kt[g, :, pl.ds(pl.multiple_of(c * CK, CK), CK)], ds)
        return carry

    lax.fori_loop(0, full + 1, grads, 0)
    for i in range(HP):
        cols = pl.ds(pl.multiple_of((head + i) * W, W), W)
        dq_ref[blk, :, cols] = (dq_t[:, i * W : (i + 1) * W] * SCALE).T.astype(BF16)


def fused_kernel(
    rows_ref, x_ref, q_ref, k_ref, v_ref, do_ref, w_ref,
    dx_ref, dk_ref, dv_ref, dw_ref,
    qbuf, dobuf, kv, kt, acc, e_scr, dp_scr, q_s, do_s, dq_t, dq,
    xbuf, xt, wg, wt, wcat, dws, core_in, y_in, s2, z_out, z_in, xh_out, xh_in,
    at_ref, inv_ref, dx_own, dx_out, dx_in, out_r, in_r, out_l, in_l, swap_out, swap_in,
    own_sem, kv_send, kv_recv, q_send, q_recv, x_send, x_recv,
    ring_send, ring_recv, wx_send, wx_recv, wz_send, wz_recv, wy_send, wy_recv, wp_send, wp_recv, wc_send, wc_recv,
    rs_send, rs_recv, swap_send, swap_recv, c_send, c_recv, y_send, y_recv, z_send, z_recv,
    xh_send, xh_recv, dx_send, dx_recv,
):
    s = lax.axis_index("seq")
    dp = lax.axis_index("dp")
    h, z = s // ZN, s % ZN
    y, xh, core = dp // 4, (dp // 2) % 2, dp % 2
    partner = {"seq": (1 - h) * ZN + z}
    right = {"seq": h * ZN + (z + 1) % ZN}
    left = {"seq": h * ZN + (z + ZN - 1) % ZN}
    y_peer = [{"dp": (y + j) % YN * 4 + xh * 2 + core} for j in range(1, YN)]
    xh_peer = {"dp": y * 4 + (1 - xh) * 2 + core}
    core_peer = {"dp": y * 4 + xh * 2 + 1 - core}
    barrier = pltpu.get_barrier_semaphore()
    peers = [partner, xh_peer, core_peer, right, left] + y_peer
    for d in peers:
        pl.semaphore_signal(barrier, inc=1, device_id=d, device_id_type=MESH)

    def remote(src, dst, ssem, rsem, d):
        return pltpu.make_async_remote_copy(src, dst, ssem, rsem, device_id=d, device_id_type=MESH)

    def cols(start, size):
        return pl.ds(pl.multiple_of(start, W), size)

    own = []

    def local(src, dst):
        c = pltpu.make_async_copy(src, dst, own_sem.at[len(own)])
        c.start()
        own.append(c)

    for g in range(2):
        for i, src in enumerate((k_ref, v_ref)):
            local(src.at[:, cols((h * 2 + g) * W, W)], kv.at[i, g, h, z])
    local(w_ref, wg.at[core, y, z, xh])
    local(x_ref, xbuf.at[h])
    for g in range(2):
        for src, buf in ((q_ref, qbuf), (do_ref, dobuf)):
            local(src.at[:, cols(h * HALF + g * 1024, 1024)], buf.at[h, :, pl.ds(g * 1024, 1024)])
    pl.semaphore_wait(barrier, len(peers))

    swaps = []
    for g in range(2):
        swaps.append([remote(src.at[:, cols(((1 - h) * 2 + g) * W, W)], kv.at[i, g, h, z],
                             kv_send.at[g, i], kv_recv.at[g, i], partner) for i, src in enumerate((k_ref, v_ref))])
    q_copies = []
    for n in range(4):
        q_copies.append([remote(src.at[:, cols((1 - h) * HALF + n * R, R)], buf.at[h, :, pl.ds(n * R, R)],
                                q_send.at[n, i], q_recv.at[n, i], partner)
                         for i, (src, buf) in enumerate(((q_ref, qbuf), (do_ref, dobuf)))])
    x_copy = remote(x_ref, xbuf.at[h], x_send, x_recv, partner)
    wx = remote(w_ref, wg.at[core, y, z, xh], wx_send, wx_recv, xh_peer)
    for c in swaps[0] + [wx] + q_copies[0] + q_copies[1] + swaps[1] + [x_copy] + q_copies[2] + q_copies[3]:
        c.start()

    def ring_at(way, step):
        return ((z + ZN - step) % ZN, right) if way == 0 else ((z + step) % ZN, left)

    def ring(g, i, way, step):
        at, to = ring_at(way, step)
        ref = kv.at[i, g, :, at]
        return remote(ref, ref, ring_send.at[g, i, way, step], ring_recv.at[g, i, way, step], to)

    def wring(way, step):
        at, to = ring_at(way, step)
        ref = wg.at[core, y, at, way] if step == 3 else wg.at[core, y, at]
        return remote(ref, ref, wz_send.at[way, step], wz_recv.at[way, step], to)

    def to_y(at, j):
        ref = wg.at[core, y, at]
        return remote(ref, ref, wy_send.at[at, j], wy_recv.at[at, j], y_peer[2 * j])

    def y_pass(j):
        ref = wg.at[core, (y + (3, 1)[j]) % YN, :, j]
        return remote(ref, ref, wp_send.at[j], wp_recv.at[j], y_peer[2 * j])

    def ring_start(g, i):
        swaps[g][i].wait_recv()
        for way in range(2):
            ring(g, i, way, 0).start()

    def ring_step(g, i, step):
        for way in range(2):
            if step < HOPS[i][way]:
                ring(g, i, way, step).wait_recv()
                if step + 1 < HOPS[i][way]:
                    ring(g, i, way, step + 1).start()

    def w_to_y(at):
        for j in range(2):
            to_y(at, j).start()

    def w_start():
        wx.wait_recv()
        for way in range(2):
            wring(way, 0).start()
        w_to_y(z)

    def w_step(step):
        for way in range(2):
            wring(way, step).wait_recv()
            if step < 3:
                wring(way, step + 1).start()
                w_to_y((z + ZN - 1 - step) % ZN if way == 0 else (z + 1 + step) % ZN)
        if step == 3:
            w_to_y((z + 4) % ZN)

    def w_pass():
        def one(i, carry):
            for j in range(2):
                to_y(i, j).wait_recv()
            return carry

        lax.fori_loop(0, ZN, one, 0)
        for j in range(2):
            y_pass(j).start()

    w_core = remote(wg.at[core], wg.at[core], wc_send, wc_recv, core_peer)

    def w_swap():
        for j in range(2):
            y_pass(j).wait_recv()
        w_core.start()

    def turn_keys(g):
        def one(b, carry):
            kt[g, :, cols(b * W, W)] = kv[0, g, b // ZN, b % ZN].T
            return carry

        lax.fori_loop(0, 2 * ZN, one, 0)

    def turn_x(blk):
        def one(r, carry):
            xt[r, blk] = xbuf[blk, :, cols(r * W, W)].T
            return carry

        lax.fori_loop(0, RTILES, one, 0)

    for c in range(16):
        at_ref[c] = 0
    for c in own[:5]:
        c.wait()
    ring_start(0, 0)
    ring_start(0, 1)
    def find(r, carry):
        for c in range(16):
            k = at_ref[c]
            last = jnp.minimum(k, KEEP - 1)
            kept = (k < KEEP) & (rows_ref[h * 16 + c, last] == r)
            at_ref[c] = k + kept.astype(jnp.int32)
            inv_ref[r * 16 + c] = jnp.where(kept, c * KEEP + last, -1)
        return carry

    acc[...] = jnp.zeros_like(acc)
    own[5].wait()
    for step in range(4):
        ring_step(0, 0, step)
        ring_step(0, 1, step)
        if step == 1:
            turn_x(h)
        if step < 3:
            lax.fori_loop(step * 7, min(step * 7 + 7, RTILES), find, 0)
        if step == 0:
            w_start()
        else:
            w_step(step - 1)
        if step == 2:
            ring_start(1, 0)
            ring_start(1, 1)
    turn_keys(0)
    for c in own[6:]:
        c.wait()

    def piece(g, i, hl, d):
        return acc[i, g, cols((hl * ZN + d) * W, W), :] * (SCALE if i == 0 else 1.0)

    def rs(g, i, way, step):
        src, dst, to = ((out_r, in_r, right), (out_l, in_l, left))[way]
        return remote(src.at[g, step, i], dst.at[g, step, i],
                      rs_send.at[g, i, way, step], rs_recv.at[g, i, way, step], to)

    def rs_step(g, step):
        for i in range(2):
            for way in range(2):
                n = HOPS[i][way]
                if step >= n:
                    continue
                src, dst = ((out_r, in_r), (out_l, in_l))[way]
                d = (z + n - step) % ZN if way == 0 else (z + ZN - n + step) % ZN
                if step > 0:
                    rs(g, i, way, step - 1).wait_recv()
                for hl in range(2):
                    v = piece(g, i, hl, d)
                    if step > 0:
                        v = v + dst[g, step - 1, i, hl].astype(F32)
                    src[g, step, i, hl] = v.astype(BF16)
                rs(g, i, way, step).start()

    def pair(g):
        return remote(swap_out.at[g], swap_in.at[g], swap_send.at[g], swap_recv.at[g], partner)

    def rs_end(g):
        for i, out in enumerate((dk_ref, dv_ref)):
            for way in range(2):
                rs(g, i, way, HOPS[i][way] - 1).wait_recv()
            both = [piece(g, i, hl, z) + in_r[g, HOPS[i][0] - 1, i, hl].astype(F32)
                    + in_l[g, HOPS[i][1] - 1, i, hl].astype(F32) for hl in range(2)]
            out[:, cols((h * 2 + g) * W, W)] = jnp.where(h == 0, both[0], both[1]).astype(BF16)
            swap_out[g, i] = jnp.where(h == 0, both[1], both[0]).astype(BF16)
        pair(g).start()

    def rs_out(g):
        pair(g).wait_recv()
        for i, out in enumerate((dk_ref, dv_ref)):
            out[:, cols(((1 - h) * 2 + g) * W, W)] = swap_in[g, i]

    def dw_tiles(p):
        for n in range(2):
            c = p * 2 + n
            xs = jnp.concatenate(
                [jnp.concatenate([xt[rows_ref[h * 16 + c, k], b] for b in range(2)], axis=1) for k in range(KEEP)],
                axis=0)
            out = dot(xs, dq[:, :, cols(c * W, W)].reshape(2 * W, W))
            out = out.reshape(KEEP, YN, 2, 2, 8, W)
            for cc in range(2):
                for yy in range(YN):
                    dws[p, cc, yy, pl.ds(n * KEEP, KEEP)] = out[:, yy, :, cc].reshape(KEEP, 16, W).astype(BF16)
        to_core(p).start()

    def to_core(p):
        return remote(dws.at[p, 1 - core], core_in.at[p], c_send.at[p], c_recv.at[p], core_peer)

    def dw_y(p, j):
        return remote(dws.at[p, core, (y + j + 1) % YN], y_in.at[p, j], y_send.at[p, j], y_recv.at[p, j], y_peer[j])

    def dw_to_y(p):
        to_core(p).wait_recv()
        for j in (1, 0, 2):
            yy = (y + j + 1) % YN
            dws[p, core, yy] = (dws[p, core, yy].astype(F32) + core_in[p, yy].astype(F32)).astype(BF16)
            dw_y(p, j).start()
        dws[p, core, y] = (dws[p, core, y].astype(F32) + core_in[p, y].astype(F32)).astype(BF16)

    def dw_sum(p):
        v = dws[p, core, y].astype(F32)
        for j in range(3):
            dw_y(p, j).wait_recv()
            v = v + y_in[p, j].astype(F32)
        s2[p] = v.astype(BF16)

    def dw_z(i, way, step):
        return remote(z_out.at[i, way, step], z_in.at[i, way, step],
                      z_send.at[i, way, step], z_recv.at[i, way, step], (right, left)[way])

    def half(i):
        return slice(i * KEEP, (i + 1) * KEEP)

    def dw_ring(step):
        for i in range(2):
            for way in range(2):
                n = HOPS[i][way]
                if step >= n:
                    continue
                d = (z + n - step) % ZN if way == 0 else (z + ZN - n + step) % ZN
                if step == 0:
                    z_out[i, way, step] = s2[d, half(i)]
                else:
                    dw_z(i, way, step - 1).wait_recv()
                    v = s2[d, half(i)].astype(F32) + z_in[i, way, step - 1].astype(F32)
                    z_out[i, way, step] = v.astype(BF16)
                dw_z(i, way, step).start()

    xh_copy = remote(xh_out, xh_in, xh_send, xh_recv, xh_peer)

    def dw_to_x():
        for i in range(2):
            total = s2[z, half(i)].astype(F32)
            for way in range(2):
                dw_z(i, way, HOPS[i][way] - 1).wait_recv()
                total = total + z_in[i, way, HOPS[i][way] - 1].astype(F32)
            low, high = total[:, :8], total[:, 8:]
            dw_ref[half(i)] = jnp.where(xh == 0, low, high)
            xh_out[half(i)] = jnp.where(xh == 0, high, low)
        xh_copy.start()

    def dw_end():
        xh_copy.wait_recv()
        dw_ref[...] += xh_in[...]

    def when(cond, f):
        pl.when(cond)(f)

    def q_wait(g):
        for c in q_copies[g]:
            c.wait_recv()

    def x_ready():
        x_copy.wait_recv()
        turn_x(1 - h)

    def assemble(i, carry):
        zz, m = i // (TZ // 2), i % (TZ // 2)
        v = wg[:, :, zz, :, pl.ds(pl.multiple_of(m * 16, 16), 16), :].astype(F32).reshape(2, YN, 2, 2, 8, W)
        v = v.transpose(3, 1, 2, 0, 4, 5).reshape(2, W, W)
        wt[pl.ds(zz * TZ + m * 2, 2)] = v.astype(BF16)
        return carry

    def weights_ready():
        w_core.wait_recv()
        lax.fori_loop(0, ZN * TZ // 2, assemble, 0)

    plan = {
        1: [(ring_step, 1, 0, 0), (ring_step, 1, 1, 0)],
        2: [(w_step, 3)],
        3: [(q_wait, 0)],
        4: [(ring_step, 1, 0, 1), (ring_step, 1, 1, 1)],
        7: [(ring_step, 1, 0, 2), (ring_step, 1, 1, 2)],
        9: [(q_wait, 1), (w_pass,)],
        10: [(x_ready,), (dw_tiles, 0), (dw_tiles, 1)],
        11: [(ring_step, 1, 0, 3), (ring_step, 1, 1, 3)],
        12: [(rs_step, 0, 0), (turn_keys, 1), (dw_tiles, 2), (dw_tiles, 3)],
        13: [(dw_to_y, 0), (dw_to_y, 1)],
        15: [(q_wait, 2), (rs_step, 0, 1), (dw_to_y, 2), (dw_to_y, 3)],
        17: [(w_swap,)],
        18: [(rs_step, 0, 2), (dw_tiles, 4), (dw_tiles, 5)],
        21: [(q_wait, 3), (rs_step, 0, 3), (dw_to_y, 4), (dw_to_y, 5)],
    }

    def work(it, carry):
        def tick(phase):
            for slot, steps in plan.items():
                if slot % 3 == phase:

                    @pl.when(it == slot // 3)
                    def _():
                        for f, *rest in steps:
                            f(*rest)

        theirs, quarter = it % 2, it // 2
        attend(it // 4, jnp.where(theirs == 0, h, 1 - h), quarter * HP, z,
               qbuf, dobuf, kv, kt, acc, e_scr, dp_scr, q_s, do_s, dq_t, dq, tick)
        return carry

    lax.fori_loop(0, 8, work, 0)

    def dx_part(r2):
        part = cols(r2 * 2 * W, 2 * W)
        return remote(dx_out.at[:, part], dx_in.at[:, part], dx_send.at[r2], dx_recv.at[r2], partner)

    def dx_step(r2, carry):
        for i in range(2):
            for c in range(16):
                at = inv_ref[(r2 * 2 + i) * 16 + c]
                tile = wt[jnp.maximum(at, 0)]
                wcat[i * W : (i + 1) * W, c * W : (c + 1) * W] = jnp.where(at >= 0, tile, jnp.zeros_like(tile))
        part = cols(r2 * 2 * W, 2 * W)
        out = dot_t(dq[...].reshape(2 * W, HALF), wcat[...])
        first, second = out[:W], out[W:]
        dx_out[:, part] = jnp.where(h == 0, second, first).astype(BF16)
        dx_part(r2).start()
        dx_own[:, part] = jnp.where(h == 0, first, second)
        return carry

    def dx_end(r2, carry):
        dx_part(r2).wait_recv()
        part = cols(r2 * 2 * W, 2 * W)
        dx_ref[:, part] = (dx_own[:, part] + dx_in[:, part].astype(F32)).astype(BF16)
        return carry

    rs_step(1, 0)
    dw_tiles(6)
    dw_tiles(7)
    for p in range(4):
        dw_sum(p)
    dw_to_y(6)
    dw_to_y(7)
    rs_end(0)
    rs_step(1, 1)
    weights_ready()
    lax.fori_loop(0, 3, dx_step, 0)
    dw_sum(4)
    dw_sum(5)
    rs_step(1, 2)
    lax.fori_loop(3, 5, dx_step, 0)
    dw_sum(6)
    dw_sum(7)
    dw_ring(0)
    rs_step(1, 3)
    lax.fori_loop(5, 7, dx_step, 0)
    dw_ring(1)
    rs_end(1)
    lax.fori_loop(7, 9, dx_step, 0)
    dw_ring(2)
    lax.fori_loop(9, 10, dx_step, 0)
    rs_out(0)
    dw_ring(3)
    rs_out(1)
    dw_to_x()
    lax.fori_loop(0, 10, dx_end, 0)
    dw_end()

    for c in swaps[0] + swaps[1] + sum(q_copies, []) + [x_copy, wx, w_core, xh_copy]:
        c.wait_send()
    for way in range(2):
        for step in range(4):
            wring(way, step).wait_send()
            for i in range(2):
                if step < HOPS[i][way]:
                    ring(0, i, way, step).wait_send()
                    ring(1, i, way, step).wait_send()
        y_pass(way).wait_send()
    for g in range(2):
        for i in range(2):
            for way in range(2):
                for step in range(HOPS[i][way]):
                    rs(g, i, way, step).wait_send()
        pair(g).wait_send()

    def sent_w(i, carry):
        for j in range(2):
            to_y(i, j).wait_send()
        return carry

    lax.fori_loop(0, ZN, sent_w, 0)

    def sent_dw(p, carry):
        to_core(p).wait_send()
        for j in range(3):
            dw_y(p, j).wait_send()
        return carry

    lax.fori_loop(0, ZN, sent_dw, 0)
    for i in range(2):
        for way in range(2):
            for step in range(HOPS[i][way]):
                dw_z(i, way, step).wait_send()

    def sent_dx(r2, carry):
        dx_part(r2).wait_send()
        return carry

    lax.fori_loop(0, 10, sent_dx, 0)


def fused(rows, x, q, k, v, do, w):
    any_spec = pl.BlockSpec(memory_space=pl.ANY)
    vmem = pl.BlockSpec(memory_space=pltpu.VMEM)
    smem = pl.BlockSpec(memory_space=pltpu.SMEM)
    dma = pltpu.SemaphoreType.DMA

    def low(*shape):
        return pltpu.VMEM(shape, BF16)

    def full(*shape):
        return pltpu.VMEM(shape, F32)

    return pl.pallas_call(
        fused_kernel,
        out_shape=(
            jax.ShapeDtypeStruct((W, D), BF16),
            jax.ShapeDtypeStruct((W, 512), BF16),
            jax.ShapeDtypeStruct((W, 512), BF16),
            jax.ShapeDtypeStruct((TZ, 8, W), F32),
        ),
        in_specs=[smem] + [any_spec] * 6,
        out_specs=(vmem,) * 4,
        scratch_shapes=[
            low(2, W, HALF), low(2, W, HALF), low(2, 2, 2, ZN, W, W), low(2, W, 2048), full(2, 2, 2048, W),
            full(2048, R), full(2048, R), low(R, W), low(R, W), full(W, R), low(2, W, HALF),
            low(2, W, D), low(RTILES, 2, W, W), low(2, YN, ZN, 2, TZ * 8, W), low(ZN * TZ, W, W), low(2 * W, HALF),
            low(ZN, 2, YN, TZ, 16, W), low(ZN, YN, TZ, 16, W), low(ZN, 3, TZ, 16, W), low(ZN, TZ, 16, W),
            low(2, 2, 4, KEEP, 16, W), low(2, 2, 4, KEEP, 16, W), full(TZ, 8, W), full(TZ, 8, W),
            pltpu.SMEM((16,), jnp.int32), pltpu.SMEM((RTILES * 16,), jnp.int32), full(W, D), low(W, D), low(W, D),
            low(2, 4, 2, 2, W, W), low(2, 4, 2, 2, W, W), low(2, 4, 2, 2, W, W), low(2, 4, 2, 2, W, W),
            low(2, 2, W, W), low(2, 2, W, W),
            dma((10,)), dma((2, 2)), dma((2, 2)), dma((4, 2)), dma((4, 2)), dma, dma,
            dma((2, 2, 2, 4)), dma((2, 2, 2, 4)), dma, dma, dma((2, 4)), dma((2, 4)), dma((ZN, 2)), dma((ZN, 2)), dma((2,)), dma((2,)),
            dma, dma,
            dma((2, 2, 2, 4)), dma((2, 2, 2, 4)), dma((2,)), dma((2,)), dma((ZN,)), dma((ZN,)), dma((ZN, 3)), dma((ZN, 3)),
            dma((2, 2, 4)), dma((2, 2, 4)), dma, dma, dma((10,)), dma((10,)),
        ],
        compiler_params=pltpu.CompilerParams(
            collective_id=0, has_side_effects=True, vmem_limit_bytes=VMEM_LIMIT
        ),
        cost_estimate=pl.CostEstimate(flops=14 * 10**9, bytes_accessed=8 * 10**6, transcendentals=10**7),
    )(rows, x, q, k, v, do, w)


def body(x, q, k, v, do, w, tile_rows, loss_scale):
    dx, dk, dv, dw = fused(
        tile_rows, x[0], q[0], k[0], v[0], do[0], w.reshape(TZ * 8, W))
    return dx[None], dk[None], dv[None], dw / loss_scale[0].astype(F32)


def solution(mesh):
    tokens = P("dp", "seq", None)
    tiles = P("seq", "dp", None)
    return jax.shard_map(
        body,
        mesh=mesh,
        in_specs=(tokens,) * 5 + (tiles, P(), P()),
        out_specs=(tokens, tokens, tokens, tiles),
        check_vma=False,
    )
```

```python
import functools

import jax
import jax.numpy as jnp
from jax import lax
from jax.experimental import pallas as pl
from jax.experimental.pallas import tpu as pltpu
from jax.sharding import PartitionSpec as P

D = 2560
W = 128
KEEP = 10
RTILES = 20
ZN = 8
HALF = 2048
HP = 4
R = HP * W
CK = 1024
KB = CK // W
YN = 4
HOPS = ((4, 3), (3, 4))
TZ = 20
SCALE = W**-0.5
VMEM_LIMIT = 60 * 2**20
EXP_SCALE = SCALE * 1.4426950408889634
MESH = pl.DeviceIdType.MESH
F32 = jnp.float32
BF16 = jnp.bfloat16


def dot_t(a, b):
    return lax.dot_general(a, b, (((1,), (1,)), ((), ())), preferred_element_type=F32)


def dot(a, b):
    return lax.dot_general(a, b, (((1,), (0,)), ((), ())), preferred_element_type=F32)


def fold(x, op):
    return op(x.reshape(x.shape[0] // 8, 8, x.shape[1]), axis=0)


def attend(g, blk, head, z, qbuf, dobuf, kv, kt, acc, e_scr, dp_scr, q_s, do_s, dq_t, dq_ref, tick):
    tick(0)
    for i in range(HP):
        cols = pl.ds(pl.multiple_of((head + i) * W, W), W)
        q_s[i * W : (i + 1) * W, :] = qbuf[blk, :, cols]
        do_s[i * W : (i + 1) * W, :] = dobuf[blk, :, cols]
    t = blk * ZN + z
    full = t // KB

    def chunk(ref, c):
        return kv[ref, g, c // (ZN // KB), pl.ds((c % (ZN // KB)) * KB, KB)].reshape(CK, W)

    def rows(c):
        return pl.ds(pl.multiple_of(c * CK, CK), CK)

    def scores(c, top):
        s = dot_t(chunk(0, c), q_s[...])
        e_scr[rows(c), :] = s
        return jnp.maximum(top, fold(s, jnp.max))

    top = lax.fori_loop(0, full, scores, jnp.full((8, R), -1e30, F32))
    s = dot_t(chunk(0, full), q_s[...])
    key = full * CK + lax.broadcasted_iota(jnp.int32, (CK, R), 0)
    pos = t * W + lax.broadcasted_iota(jnp.int32, (CK, R), 1) % W
    s = jnp.where(key <= pos, s, -1e30)
    e_scr[rows(full), :] = s
    top = jnp.max(jnp.maximum(top, fold(s, jnp.max)), axis=0, keepdims=True)

    tick(1)

    def exps(c, carry):
        total, weighted = carry
        e = jnp.exp2((e_scr[rows(c), :] - top) * EXP_SCALE)
        dp = dot_t(chunk(1, c), do_s[...])
        e_scr[rows(c), :] = e
        dp_scr[rows(c), :] = dp
        return total + fold(e, jnp.sum), weighted + fold(e * dp, jnp.sum)

    zero = jnp.zeros((8, R), F32)
    total, weighted = lax.fori_loop(0, full + 1, exps, (zero, zero))
    inv = 1.0 / jnp.sum(total, axis=0, keepdims=True)
    delta = jnp.sum(weighted, axis=0, keepdims=True) * inv
    dq_t[...] = jnp.zeros_like(dq_t)
    tick(2)

    def grads(c, carry):
        p = e_scr[rows(c), :] * inv
        ds = (p * (dp_scr[rows(c), :] - delta)).astype(BF16)
        acc[0, g, rows(c), :] += dot(ds, q_s[...])
        acc[1, g, rows(c), :] += dot(p.astype(BF16), do_s[...])
        dq_t[...] += dot(kt[g, :, pl.ds(pl.multiple_of(c * CK, CK), CK)], ds)
        return carry

    lax.fori_loop(0, full + 1, grads, 0)
    for i in range(HP):
        cols = pl.ds(pl.multiple_of((head + i) * W, W), W)
        dq_ref[blk, :, cols] = (dq_t[:, i * W : (i + 1) * W] * SCALE).T.astype(BF16)


def fused_kernel(
    rows_ref, x_ref, q_ref, k_ref, v_ref, do_ref, w_ref,
    dx_ref, dk_ref, dv_ref, dw_ref,
    qbuf, dobuf, kv, kt, acc, e_scr, dp_scr, q_s, do_s, dq_t, dq,
    xbuf, xt, wg, wt, wcat, dws, core_in, y_in, s2, z_out, z_in, xh_out, xh_in,
    at_ref, inv_ref, dx_own, dx_out, dx_in, out_r, in_r, out_l, in_l, swap_out, swap_in,
    own_sem, kv_send, kv_recv, q_send, q_recv, x_send, x_recv,
    ring_send, ring_recv, wx_send, wx_recv, wz_send, wz_recv, wy_send, wy_recv, wp_send, wp_recv, wc_send, wc_recv,
    rs_send, rs_recv, swap_send, swap_recv, c_send, c_recv, y_send, y_recv, z_send, z_recv,
    xh_send, xh_recv, dx_send, dx_recv,
):
    s = lax.axis_index("seq")
    dp = lax.axis_index("dp")
    h, z = s // ZN, s % ZN
    y, xh, core = dp // 4, (dp // 2) % 2, dp % 2
    partner = {"seq": (1 - h) * ZN + z}
    right = {"seq": h * ZN + (z + 1) % ZN}
    left = {"seq": h * ZN + (z + ZN - 1) % ZN}
    y_peer = [{"dp": (y + j) % YN * 4 + xh * 2 + core} for j in range(1, YN)]
    xh_peer = {"dp": y * 4 + (1 - xh) * 2 + core}
    core_peer = {"dp": y * 4 + xh * 2 + 1 - core}
    barrier = pltpu.get_barrier_semaphore()
    peers = [partner, xh_peer, core_peer, right, left] + y_peer
    for d in peers:
        pl.semaphore_signal(barrier, inc=1, device_id=d, device_id_type=MESH)

    def remote(src, dst, ssem, rsem, d):
        return pltpu.make_async_remote_copy(src, dst, ssem, rsem, device_id=d, device_id_type=MESH)

    def cols(start, size):
        return pl.ds(pl.multiple_of(start, W), size)

    own = []

    def local(src, dst):
        c = pltpu.make_async_copy(src, dst, own_sem.at[len(own)])
        c.start()
        own.append(c)

    for g in range(2):
        for i, src in enumerate((k_ref, v_ref)):
            local(src.at[:, cols((h * 2 + g) * W, W)], kv.at[i, g, h, z])
    local(w_ref, wg.at[core, y, z, xh])
    local(x_ref, xbuf.at[h])
    for g in range(2):
        for src, buf in ((q_ref, qbuf), (do_ref, dobuf)):
            local(src.at[:, cols(h * HALF + g * 1024, 1024)], buf.at[h, :, pl.ds(g * 1024, 1024)])
    pl.semaphore_wait(barrier, len(peers))

    swaps = []
    for g in range(2):
        swaps.append([remote(src.at[:, cols(((1 - h) * 2 + g) * W, W)], kv.at[i, g, h, z],
                             kv_send.at[g, i], kv_recv.at[g, i], partner) for i, src in enumerate((k_ref, v_ref))])
    q_copies = []
    for n in range(4):
        q_copies.append([remote(src.at[:, cols((1 - h) * HALF + n * R, R)], buf.at[h, :, pl.ds(n * R, R)],
                                q_send.at[n, i], q_recv.at[n, i], partner)
                         for i, (src, buf) in enumerate(((q_ref, qbuf), (do_ref, dobuf)))])
    x_copy = remote(x_ref, xbuf.at[h], x_send, x_recv, partner)
    wx = remote(w_ref, wg.at[core, y, z, xh], wx_send, wx_recv, xh_peer)
    for c in swaps[0] + [wx] + q_copies[0] + q_copies[1] + swaps[1] + [x_copy] + q_copies[2] + q_copies[3]:
        c.start()

    def ring_at(way, step):
        return ((z + ZN - step) % ZN, right) if way == 0 else ((z + step) % ZN, left)

    def ring(g, i, way, step):
        at, to = ring_at(way, step)
        ref = kv.at[i, g, :, at]
        return remote(ref, ref, ring_send.at[g, i, way, step], ring_recv.at[g, i, way, step], to)

    def wring(way, step):
        at, to = ring_at(way, step)
        ref = wg.at[core, y, at, way] if step == 3 else wg.at[core, y, at]
        return remote(ref, ref, wz_send.at[way, step], wz_recv.at[way, step], to)

    def to_y(at, j):
        ref = wg.at[core, y, at]
        return remote(ref, ref, wy_send.at[at, j], wy_recv.at[at, j], y_peer[2 * j])

    def y_pass(j):
        ref = wg.at[core, (y + (3, 1)[j]) % YN, :, j]
        return remote(ref, ref, wp_send.at[j], wp_recv.at[j], y_peer[2 * j])

    def ring_start(g, i):
        swaps[g][i].wait_recv()
        for way in range(2):
            ring(g, i, way, 0).start()

    def ring_step(g, i, step):
        for way in range(2):
            if step < HOPS[i][way]:
                ring(g, i, way, step).wait_recv()
                if step + 1 < HOPS[i][way]:
                    ring(g, i, way, step + 1).start()

    def w_to_y(at):
        for j in range(2):
            to_y(at, j).start()

    def w_start():
        wx.wait_recv()
        for way in range(2):
            wring(way, 0).start()
        w_to_y(z)

    def w_step(step):
        for way in range(2):
            wring(way, step).wait_recv()
            if step < 3:
                wring(way, step + 1).start()
                w_to_y((z + ZN - 1 - step) % ZN if way == 0 else (z + 1 + step) % ZN)
        if step == 3:
            w_to_y((z + 4) % ZN)

    def w_pass():
        def one(i, carry):
            for j in range(2):
                to_y(i, j).wait_recv()
            return carry

        lax.fori_loop(0, ZN, one, 0)
        for j in range(2):
            y_pass(j).start()

    w_core = remote(wg.at[core], wg.at[core], wc_send, wc_recv, core_peer)

    def w_swap():
        for j in range(2):
            y_pass(j).wait_recv()
        w_core.start()

    def turn_keys(g):
        def one(b, carry):
            kt[g, :, cols(b * W, W)] = kv[0, g, b // ZN, b % ZN].T
            return carry

        lax.fori_loop(0, 2 * ZN, one, 0)

    def turn_x(blk):
        def one(r, carry):
            xt[r, blk] = xbuf[blk, :, cols(r * W, W)].T
            return carry

        lax.fori_loop(0, RTILES, one, 0)

    for c in range(16):
        at_ref[c] = 0
    for c in own[:5]:
        c.wait()
    ring_start(0, 0)
    ring_start(0, 1)
    def find(r, carry):
        for c in range(16):
            k = at_ref[c]
            last = jnp.minimum(k, KEEP - 1)
            kept = (k < KEEP) & (rows_ref[h * 16 + c, last] == r)
            at_ref[c] = k + kept.astype(jnp.int32)
            inv_ref[r * 16 + c] = jnp.where(kept, c * KEEP + last, -1)
        return carry

    acc[...] = jnp.zeros_like(acc)
    own[5].wait()
    for step in range(4):
        ring_step(0, 0, step)
        ring_step(0, 1, step)
        if step == 1:
            turn_x(h)
        if step < 3:
            lax.fori_loop(step * 7, min(step * 7 + 7, RTILES), find, 0)
        if step == 0:
            w_start()
        else:
            w_step(step - 1)
        if step == 2:
            ring_start(1, 0)
            ring_start(1, 1)
    turn_keys(0)
    for c in own[6:]:
        c.wait()

    def piece(g, i, hl, d):
        return acc[i, g, cols((hl * ZN + d) * W, W), :] * (SCALE if i == 0 else 1.0)

    def rs(g, i, way, step):
        src, dst, to = ((out_r, in_r, right), (out_l, in_l, left))[way]
        return remote(src.at[g, step, i], dst.at[g, step, i],
                      rs_send.at[g, i, way, step], rs_recv.at[g, i, way, step], to)

    def rs_step(g, step):
        for i in range(2):
            for way in range(2):
                n = HOPS[i][way]
                if step >= n:
                    continue
                src, dst = ((out_r, in_r), (out_l, in_l))[way]
                d = (z + n - step) % ZN if way == 0 else (z + ZN - n + step) % ZN
                if step > 0:
                    rs(g, i, way, step - 1).wait_recv()
                for hl in range(2):
                    v = piece(g, i, hl, d)
                    if step > 0:
                        v = v + dst[g, step - 1, i, hl].astype(F32)
                    src[g, step, i, hl] = v.astype(BF16)
                rs(g, i, way, step).start()

    def pair(g):
        return remote(swap_out.at[g], swap_in.at[g], swap_send.at[g], swap_recv.at[g], partner)

    def rs_end(g):
        for i, out in enumerate((dk_ref, dv_ref)):
            for way in range(2):
                rs(g, i, way, HOPS[i][way] - 1).wait_recv()
            both = [piece(g, i, hl, z) + in_r[g, HOPS[i][0] - 1, i, hl].astype(F32)
                    + in_l[g, HOPS[i][1] - 1, i, hl].astype(F32) for hl in range(2)]
            out[:, cols((h * 2 + g) * W, W)] = jnp.where(h == 0, both[0], both[1]).astype(BF16)
            swap_out[g, i] = jnp.where(h == 0, both[1], both[0]).astype(BF16)
        pair(g).start()

    def rs_out(g):
        pair(g).wait_recv()
        for i, out in enumerate((dk_ref, dv_ref)):
            out[:, cols(((1 - h) * 2 + g) * W, W)] = swap_in[g, i]

    def dw_tiles(p):
        for n in range(2):
            c = p * 2 + n
            xs = jnp.concatenate(
                [jnp.concatenate([xt[rows_ref[h * 16 + c, k], b] for b in range(2)], axis=1) for k in range(KEEP)],
                axis=0)
            out = dot(xs, dq[:, :, cols(c * W, W)].reshape(2 * W, W))
            out = out.reshape(KEEP, YN, 2, 2, 8, W)
            for cc in range(2):
                for yy in range(YN):
                    dws[p, cc, yy, pl.ds(n * KEEP, KEEP)] = out[:, yy, :, cc].reshape(KEEP, 16, W).astype(BF16)
        to_core(p).start()

    def to_core(p):
        return remote(dws.at[p, 1 - core], core_in.at[p], c_send.at[p], c_recv.at[p], core_peer)

    def dw_y(p, j):
        return remote(dws.at[p, core, (y + j + 1) % YN], y_in.at[p, j], y_send.at[p, j], y_recv.at[p, j], y_peer[j])

    def dw_to_y(p):
        to_core(p).wait_recv()
        for j in (1, 0, 2):
            yy = (y + j + 1) % YN
            dws[p, core, yy] = (dws[p, core, yy].astype(F32) + core_in[p, yy].astype(F32)).astype(BF16)
            dw_y(p, j).start()
        dws[p, core, y] = (dws[p, core, y].astype(F32) + core_in[p, y].astype(F32)).astype(BF16)

    def dw_sum(p):
        v = dws[p, core, y].astype(F32)
        for j in range(3):
            dw_y(p, j).wait_recv()
            v = v + y_in[p, j].astype(F32)
        s2[p] = v.astype(BF16)

    def dw_z(i, way, step):
        return remote(z_out.at[i, way, step], z_in.at[i, way, step],
                      z_send.at[i, way, step], z_recv.at[i, way, step], (right, left)[way])

    def half(i):
        return slice(i * KEEP, (i + 1) * KEEP)

    def dw_ring(step):
        for i in range(2):
            for way in range(2):
                n = HOPS[i][way]
                if step >= n:
                    continue
                d = (z + n - step) % ZN if way == 0 else (z + ZN - n + step) % ZN
                if step == 0:
                    z_out[i, way, step] = s2[d, half(i)]
                else:
                    dw_z(i, way, step - 1).wait_recv()
                    v = s2[d, half(i)].astype(F32) + z_in[i, way, step - 1].astype(F32)
                    z_out[i, way, step] = v.astype(BF16)
                dw_z(i, way, step).start()

    xh_copies = [remote(xh_out.at[pl.ds(i * KEEP, KEEP)], xh_in.at[pl.ds(i * KEEP, KEEP)],
                        xh_send.at[i], xh_recv.at[i], xh_peer) for i in range(2)]

    def dw_to_x():
        for i in range(2):
            total = s2[z, half(i)].astype(F32)
            for way in range(2):
                dw_z(i, way, HOPS[i][way] - 1).wait_recv()
                total = total + z_in[i, way, HOPS[i][way] - 1].astype(F32)
            low, high = total[:, :8], total[:, 8:]
            dw_ref[half(i)] = jnp.where(xh == 0, low, high)
            xh_out[half(i)] = jnp.where(xh == 0, high, low)
            xh_copies[i].start()

    def dw_end():
        for i in range(2):
            xh_copies[i].wait_recv()
            dw_ref[half(i)] += xh_in[half(i)]

    def when(cond, f):
        pl.when(cond)(f)

    def q_wait(g):
        for c in q_copies[g]:
            c.wait_recv()

    def x_ready():
        x_copy.wait_recv()
        turn_x(1 - h)

    def assemble(i, carry):
        zz, m = i // (TZ // 2), i % (TZ // 2)
        v = wg[:, :, zz, :, pl.ds(pl.multiple_of(m * 16, 16), 16), :].astype(F32).reshape(2, YN, 2, 2, 8, W)
        v = v.transpose(3, 1, 2, 0, 4, 5).reshape(2, W, W)
        wt[pl.ds(zz * TZ + m * 2, 2)] = v.astype(BF16)
        return carry

    def weights_ready():
        w_core.wait_recv()
        lax.fori_loop(0, ZN * TZ // 2, assemble, 0)

    plan = {
        1: [(ring_step, 1, 0, 0), (ring_step, 1, 1, 0)],
        2: [(w_step, 3)],
        3: [(q_wait, 0)],
        4: [(ring_step, 1, 0, 1), (ring_step, 1, 1, 1)],
        7: [(ring_step, 1, 0, 2), (ring_step, 1, 1, 2)],
        9: [(q_wait, 1), (w_pass,)],
        10: [(x_ready,), (dw_tiles, 0), (dw_tiles, 1)],
        11: [(ring_step, 1, 0, 3), (ring_step, 1, 1, 3)],
        12: [(rs_step, 0, 0), (turn_keys, 1), (dw_tiles, 2), (dw_tiles, 3)],
        13: [(dw_to_y, 0), (dw_to_y, 1)],
        15: [(q_wait, 2), (rs_step, 0, 1), (dw_to_y, 2), (dw_to_y, 3)],
        17: [(w_swap,)],
        18: [(rs_step, 0, 2), (dw_tiles, 4), (dw_tiles, 5)],
        20: [(dw_to_y, 4), (dw_to_y, 5)],
        21: [(q_wait, 3), (rs_step, 0, 3)],
    }

    def work(it, carry):
        def tick(phase):
            for slot, steps in plan.items():
                if slot % 3 == phase:

                    @pl.when(it == slot // 3)
                    def _():
                        for f, *rest in steps:
                            f(*rest)

        theirs, quarter = it % 2, it // 2
        attend(it // 4, jnp.where(theirs == 0, h, 1 - h), quarter * HP, z,
               qbuf, dobuf, kv, kt, acc, e_scr, dp_scr, q_s, do_s, dq_t, dq, tick)
        return carry

    lax.fori_loop(0, 8, work, 0)

    def dx_part(r2):
        part = cols(r2 * 2 * W, 2 * W)
        return remote(dx_out.at[:, part], dx_in.at[:, part], dx_send.at[r2], dx_recv.at[r2], partner)

    def dx_step(r2, carry):
        for i in range(2):
            for c in range(16):
                at = inv_ref[(r2 * 2 + i) * 16 + c]
                tile = wt[jnp.maximum(at, 0)]
                wcat[i * W : (i + 1) * W, c * W : (c + 1) * W] = jnp.where(at >= 0, tile, jnp.zeros_like(tile))
        part = cols(r2 * 2 * W, 2 * W)
        out = dot_t(dq[...].reshape(2 * W, HALF), wcat[...])
        first, second = out[:W], out[W:]
        dx_out[:, part] = jnp.where(h == 0, second, first).astype(BF16)
        dx_part(r2).start()
        dx_own[:, part] = jnp.where(h == 0, first, second)
        return carry

    def dx_end(r2, carry):
        dx_part(r2).wait_recv()
        part = cols(r2 * 2 * W, 2 * W)
        dx_ref[:, part] = (dx_own[:, part] + dx_in[:, part].astype(F32)).astype(BF16)
        return carry

    dw_tiles(6)
    dw_tiles(7)
    rs_step(1, 0)
    for p in range(4):
        dw_sum(p)
    dw_to_y(6)
    dw_to_y(7)
    rs_end(0)
    weights_ready()
    rs_step(1, 1)
    lax.fori_loop(0, 3, dx_step, 0)
    dw_sum(4)
    dw_sum(5)
    rs_step(1, 2)
    dw_sum(6)
    dw_sum(7)
    dw_ring(0)
    lax.fori_loop(3, 5, dx_step, 0)
    rs_step(1, 3)
    dw_ring(1)
    lax.fori_loop(5, 7, dx_step, 0)
    dw_ring(2)
    rs_end(1)
    lax.fori_loop(7, 10, dx_step, 0)
    dw_ring(3)
    rs_out(0)
    rs_out(1)
    dw_to_x()
    lax.fori_loop(0, 10, dx_end, 0)
    dw_end()

    for c in swaps[0] + swaps[1] + sum(q_copies, []) + xh_copies + [x_copy, wx, w_core]:
        c.wait_send()
    for way in range(2):
        for step in range(4):
            wring(way, step).wait_send()
            for i in range(2):
                if step < HOPS[i][way]:
                    ring(0, i, way, step).wait_send()
                    ring(1, i, way, step).wait_send()
        y_pass(way).wait_send()
    for g in range(2):
        for i in range(2):
            for way in range(2):
                for step in range(HOPS[i][way]):
                    rs(g, i, way, step).wait_send()
        pair(g).wait_send()

    def sent_w(i, carry):
        for j in range(2):
            to_y(i, j).wait_send()
        return carry

    lax.fori_loop(0, ZN, sent_w, 0)

    def sent_dw(p, carry):
        to_core(p).wait_send()
        for j in range(3):
            dw_y(p, j).wait_send()
        return carry

    lax.fori_loop(0, ZN, sent_dw, 0)
    for i in range(2):
        for way in range(2):
            for step in range(HOPS[i][way]):
                dw_z(i, way, step).wait_send()

    def sent_dx(r2, carry):
        dx_part(r2).wait_send()
        return carry

    lax.fori_loop(0, 10, sent_dx, 0)


def fused(rows, x, q, k, v, do, w):
    any_spec = pl.BlockSpec(memory_space=pl.ANY)
    vmem = pl.BlockSpec(memory_space=pltpu.VMEM)
    smem = pl.BlockSpec(memory_space=pltpu.SMEM)
    dma = pltpu.SemaphoreType.DMA

    def low(*shape):
        return pltpu.VMEM(shape, BF16)

    def full(*shape):
        return pltpu.VMEM(shape, F32)

    return pl.pallas_call(
        fused_kernel,
        out_shape=(
            jax.ShapeDtypeStruct((W, D), BF16),
            jax.ShapeDtypeStruct((W, 512), BF16),
            jax.ShapeDtypeStruct((W, 512), BF16),
            jax.ShapeDtypeStruct((TZ, 8, W), F32),
        ),
        in_specs=[smem] + [any_spec] * 6,
        out_specs=(vmem,) * 4,
        scratch_shapes=[
            low(2, W, HALF), low(2, W, HALF), low(2, 2, 2, ZN, W, W), low(2, W, 2048), full(2, 2, 2048, W),
            full(2048, R), full(2048, R), low(R, W), low(R, W), full(W, R), low(2, W, HALF),
            low(2, W, D), low(RTILES, 2, W, W), low(2, YN, ZN, 2, TZ * 8, W), low(ZN * TZ, W, W), low(2 * W, HALF),
            low(ZN, 2, YN, TZ, 16, W), low(ZN, YN, TZ, 16, W), low(ZN, 3, TZ, 16, W), low(ZN, TZ, 16, W),
            low(2, 2, 4, KEEP, 16, W), low(2, 2, 4, KEEP, 16, W), full(TZ, 8, W), full(TZ, 8, W),
            pltpu.SMEM((16,), jnp.int32), pltpu.SMEM((RTILES * 16,), jnp.int32), full(W, D), low(W, D), low(W, D),
            low(2, 4, 2, 2, W, W), low(2, 4, 2, 2, W, W), low(2, 4, 2, 2, W, W), low(2, 4, 2, 2, W, W),
            low(2, 2, W, W), low(2, 2, W, W),
            dma((10,)), dma((2, 2)), dma((2, 2)), dma((4, 2)), dma((4, 2)), dma, dma,
            dma((2, 2, 2, 4)), dma((2, 2, 2, 4)), dma, dma, dma((2, 4)), dma((2, 4)), dma((ZN, 2)), dma((ZN, 2)), dma((2,)), dma((2,)),
            dma, dma,
            dma((2, 2, 2, 4)), dma((2, 2, 2, 4)), dma((2,)), dma((2,)), dma((ZN,)), dma((ZN,)), dma((ZN, 3)), dma((ZN, 3)),
            dma((2, 2, 4)), dma((2, 2, 4)), dma((2,)), dma((2,)), dma((10,)), dma((10,)),
        ],
        compiler_params=pltpu.CompilerParams(
            collective_id=0, has_side_effects=True, vmem_limit_bytes=VMEM_LIMIT
        ),
        cost_estimate=pl.CostEstimate(flops=14 * 10**9, bytes_accessed=8 * 10**6, transcendentals=10**7),
    )(rows, x, q, k, v, do, w)


def body(x, q, k, v, do, w, tile_rows, loss_scale):
    dx, dk, dv, dw = fused(
        tile_rows, x[0], q[0], k[0], v[0], do[0], w.reshape(TZ * 8, W))
    return dx[None], dk[None], dv[None], dw / loss_scale[0].astype(F32)


def solution(mesh):
    tokens = P("dp", "seq", None)
    tiles = P("seq", "dp", None)
    return jax.shard_map(
        body,
        mesh=mesh,
        in_specs=(tokens,) * 5 + (tiles, P(), P()),
        out_specs=(tokens, tokens, tokens, tiles),
        check_vma=False,
    )
```
